512 devices in a mesh: dp: 8 (over z), ctx: 64 (over y, x, core).
Axes of the slice: x: 4, y: 8, z: 8, core: 2. Of those that a mesh axis runs over, the one named last changes fastest.
Arguments:
- queries: bfloat16 [8, 8192, 2048], P('dp', 'ctx')
- keys: bfloat16 [8, 8192, 2048], P('dp', 'ctx')
- values: bfloat16 [8, 8192, 2048], P('dp', 'ctx'), may hold values from -6 to 6
- router_logit: float32 [8, 8192], P('dp', 'ctx'), may hold values from -8 to 8
- head_scale: float32 [16], replicated, may hold values from 0.5 to 2
- routed: int32 [8, 1024], P('dp'), may hold values from 0 to 8191, as said below
- grad_out: bfloat16 [8, 8192, 2048], P('dp', 'ctx'), may hold values from -6 to 6
Outputs:
- block_out: bfloat16 [8, 8192, 2048], P('dp', 'ctx')
- d_queries: bfloat16 [8, 8192, 2048], P('dp', 'ctx')
- d_keys: bfloat16 [8, 8192, 2048], P('dp', 'ctx')
- d_values: bfloat16 [8, 8192, 2048], P('dp', 'ctx')
- d_logit: float32 [8, 8192], P('dp', 'ctx')
- d_head_scale: float32 [16], replicated
The draws below stay inside these ranges and needn't reach their ends.
Inputs may be any that keep to these rules, and one draw needn't show every extreme that they name: Each document's routed positions increase strictly. A shard of 128 positions (positions c * 128 to c * 128 + 127) holds 1 to 40 of them, and in every document some shard holds exactly 40.
All inputs are finite; a program needn't handle non-finite values.
Results may differ from the reference program's by a relative error of at most 0.011.
Values may be sent and summed in bfloat16 or wider, within the bound.
No kernel may reach another device: no remote copies, remote signals or barrier semaphores. Data moves between devices by JAX's collectives and lax.ppermute only.
A program may use at most 128 MiB of HBM per device.

```python
import math
import jax
import jax.numpy as jnp
from jax import lax

HEADS = 16
HDIM = 128
WIDTH = 2048
TOK_DEV = 128
ROWS_DEV = 16
DOCS = 8
SEQ = 8192
ROUTED = 1024
XMAX = 8
N_CTX = 64


def shared_rows(key):
    return jax.random.truncated_normal(key, -6.0, 6.0, (DOCS, SEQ, WIDTH), jnp.float32)


def draw_keys(key, part):
    common = shared_rows(key)
    return common.astype(jnp.bfloat16)


def draw_queries(key, part):
    key = jax.random.fold_in(key, 1)
    own = jax.random.truncated_normal(key, -6.0, 6.0, (DOCS, SEQ, WIDTH), jnp.float32)
    return own.astype(jnp.bfloat16)


def routed_document(key):
    key_order, key_extra, key_pick = jax.random.split(key, 3)
    order = jax.random.permutation(key_order, N_CTX)
    groups = N_CTX // 4
    extra = jax.random.randint(key_extra, (groups,), 0, XMAX + 1)
    extra = extra.at[0].set(XMAX)
    ranked = jnp.stack([ROWS_DEV + 3 * extra, ROWS_DEV - extra, ROWS_DEV - extra, ROWS_DEV - extra], axis=1)
    counts = jnp.zeros((N_CTX,), jnp.int32).at[order].set(ranked.reshape(-1).astype(jnp.int32))
    marks = jax.random.randint(key_pick, (N_CTX, TOK_DEV), 0, 1 << 20) * TOK_DEV
    marks = marks + jnp.arange(TOK_DEV, dtype=jnp.int32)[None, :]
    rank = jnp.argsort(jnp.argsort(marks, axis=1), axis=1)
    chosen = rank < counts[:, None]
    places = jnp.nonzero(chosen.reshape(-1), size=ROUTED)[0]
    return places.astype(jnp.int32)


def draw_routed(key, part):
    key = jax.random.fold_in(key, 7)
    doc_keys = jax.random.split(key, DOCS)
    return jax.vmap(routed_document)(doc_keys)


def level_of(rng, shape, shards, least, largest):
    def one(axis_at, blocks):
        steps = jax.random.uniform(jax.random.fold_in(jax.random.fold_in(rng, 6), axis_at), (blocks,), jnp.float32, least / len(shards), largest / len(shards))
        return jnp.repeat(jnp.exp(steps), shape[axis_at] // blocks).reshape((-1,) + (1,) * (len(shape) - axis_at - 1))

    factor_of = one(*shards[0])
    for cut in shards[1:]:
        factor_of = factor_of * one(*cut)
    return factor_of


def scatter_about(own_key, extent, scale, limit, cuts=(), kind=jnp.bfloat16):
    values = jax.random.normal(own_key, extent, jnp.float32) * scale
    if len(cuts) > 0:
        values = level_of(own_key, extent, cuts, -0.22, 0.18) * values
    return jnp.clip(values, min=-limit, max=limit).astype(kind)


def setup_inputs(seed: int = 0) -> dict:
    key_list = jax.random.split(jax.random.key(seed), 8)
    queries = draw_queries(jax.random.fold_in(key_list[7], 71), 0)
    keys = draw_keys(jax.random.fold_in(key_list[7], 71), 0)
    values = scatter_about(key_list[2], (DOCS, SEQ, WIDTH), 1.0, 6.0, ((0, 8), (1, 64)))
    router_logit = scatter_about(key_list[3], (DOCS, SEQ), 2.0, 8.0, ((0, 8), (1, 64)), jnp.float32)
    head_scale = jnp.clip(jnp.exp(jax.random.uniform(key_list[4], (HEADS,), jnp.float32, math.log(0.5), math.log(2.0))), 0.5, 2.0)
    routed = draw_routed(jax.random.fold_in(key_list[7], 71), 0)
    grad_out = scatter_about(key_list[6], (DOCS, SEQ, WIDTH), 1.0, 6.0, ((0, 8), (1, 64)))
    return {"queries": queries, "keys": keys, "values": values, "router_logit": router_logit, "head_scale": head_scale, "routed": routed, "grad_out": grad_out}


def one_document(args, head_scale):
    queries, keys, values, logit, grad_out, pos = args
    count = pos.shape[0]
    inv = 1.0 / math.sqrt(HDIM)
    rows_q = queries[pos].reshape(count, HEADS, HDIM).astype(jnp.float32)
    rows_k = keys[pos].reshape(count, HEADS, HDIM).astype(jnp.float32)
    rows_v = values[pos].reshape(count, HEADS, HDIM).astype(jnp.float32)
    gate = jax.nn.sigmoid(logit[pos])
    raw = jnp.einsum('shd,khd->hsk', rows_q, rows_k) * inv
    scores = head_scale[:, None, None] * raw
    kept = (pos[None, :] <= pos[:, None])[None, :, :]
    masked = jnp.where(kept, scores, -jnp.inf)
    top = lax.optimization_barrier(jnp.max(masked, axis=-1, keepdims=True))
    lse = top + jnp.log(lax.optimization_barrier(jnp.sum(jnp.exp(masked - top), axis=-1, keepdims=True)))
    probs = jnp.where(kept, jnp.exp(masked - lse), 0.0)
    weights = probs.astype(jnp.bfloat16)
    attended = jnp.einsum('hsk,khd->shd', weights.astype(jnp.float32), rows_v).astype(jnp.bfloat16)
    attended = attended.reshape(count, HEADS * HDIM)
    grad_rows = grad_out[pos].astype(jnp.float32)
    d_rows = (gate[:, None] * grad_rows).astype(jnp.bfloat16)
    d_heads = d_rows.reshape(count, HEADS, HDIM).astype(jnp.float32)
    delta = lax.optimization_barrier(jnp.sum(d_heads * attended.reshape(count, HEADS, HDIM).astype(jnp.float32), axis=-1))
    d_probs = jnp.einsum('shd,khd->hsk', d_heads, rows_v)
    d_scores = probs * (d_probs - delta.T[:, :, None])
    d_weights = d_scores.astype(jnp.bfloat16).astype(jnp.float32)
    coef = (head_scale * inv)[None, :, None]
    d_q = (coef * jnp.einsum('hsk,khd->shd', d_weights, rows_k)).astype(jnp.bfloat16)
    d_k = (coef * jnp.einsum('hsk,shd->khd', d_weights, rows_q)).astype(jnp.bfloat16)
    d_v = jnp.einsum('hsk,shd->khd', weights.astype(jnp.float32), d_heads).astype(jnp.bfloat16)
    d_scale = lax.optimization_barrier(jnp.sum(d_scores * raw, axis=(1, 2)))
    width = HEADS * HDIM
    seq = queries.shape[0]
    zero_rows = jnp.zeros((seq, width), jnp.bfloat16)
    block_out = zero_rows.at[pos].set((gate[:, None] * attended.astype(jnp.float32)).astype(jnp.bfloat16))
    d_queries = zero_rows.at[pos].set(d_q.reshape(count, width))
    d_keys = zero_rows.at[pos].set(d_k.reshape(count, width))
    d_values = zero_rows.at[pos].set(d_v.reshape(count, width))
    route_grad = gate * (1.0 - gate) * lax.optimization_barrier(jnp.sum(grad_rows * attended.astype(jnp.float32), axis=-1))
    d_logit = jnp.zeros((seq,), jnp.float32).at[pos].set(route_grad)
    return (block_out, d_queries, d_keys, d_values, d_logit, d_scale)

def reference(queries, keys, values, router_logit, head_scale, routed, grad_out):
    results = lax.map(lambda args: one_document(args, head_scale), (queries, keys, values, router_logit, grad_out, routed))
    block_out, d_queries, d_keys, d_values, d_logit, d_scale = results
    return (block_out, d_queries, d_keys, d_values, d_logit, lax.optimization_barrier(jnp.sum(d_scale, axis=0)))
```

```python
import functools
import math

import jax
import jax.numpy as jnp
from jax import lax
from jax.experimental import pallas as pl
from jax.experimental.pallas import tpu as pltpu
from jax.sharding import PartitionSpec as P

F32 = jnp.float32
BF16 = jnp.bfloat16
VM = pl.BlockSpec(memory_space=pltpu.VMEM)
SM = pl.BlockSpec(memory_space=pltpu.SMEM)
NT = (((1,), (1,)), ((), ()))
PARTS = 4


def eye(n):
    return lax.broadcasted_iota(jnp.int32, (n, n), 0) == lax.broadcasted_iota(jnp.int32, (n, n), 1)


def to_row(col, n):
    return jnp.sum(jnp.where(eye(n), col, 0.0), axis=0, keepdims=True)


def to_col(row, n):
    return jnp.sum(jnp.where(eye(n), row, 0.0), axis=1, keepdims=True)


def slot_column(places, first, tok):
    total = places.shape[1]
    before = jnp.sum((places < first).astype(F32), axis=1, keepdims=True)
    rank = lax.broadcasted_iota(jnp.int32, (1, total), 1).astype(F32) + 1.0 - before
    here = places - first == lax.broadcasted_iota(jnp.int32, (tok, total), 0)
    return jnp.sum(jnp.where(here, rank, 0.0), axis=1, keepdims=True)


def sigmoid(x):
    return 1.0 / (1.0 + jnp.exp(-x))


def pack_kernel(here_ref, places_ref, logit_ref, q_ref, k_ref, v_ref, g_ref, out_ref):
    tok, width = q_ref.shape
    slots, hdim = out_ref.shape[1:]
    row = to_row(slot_column(places_ref[...], here_ref[0] * tok, tok), tok)
    hit = lax.broadcasted_iota(jnp.int32, (slots, tok), 0).astype(F32) + 1.0 == row
    pick = hit.astype(BF16)
    gate = jnp.sum(jnp.where(hit, sigmoid(logit_ref[...]), 0.0), axis=1, keepdims=True)
    for part, ref in enumerate((q_ref, k_ref, v_ref, g_ref)):
        for base in range(0, width, 4 * hdim):
            rows = jnp.dot(pick, ref[:, base : base + 4 * hdim], preferred_element_type=F32)
            if part == 3:
                rows = rows * gate
            rows = rows.astype(BF16)
            for i in range(4):
                head = base // hdim + i
                out_ref[head * PARTS + part] = rows[:, i * hdim : (i + 1) * hdim]


def compact_kernel(before_ref, in_ref, out_ref, buf):
    shards, slots, _ = in_ref.shape
    total = out_ref.shape[0]
    for c in range(shards):
        buf[pl.ds(before_ref[c], slots), :] = in_ref[c].astype(F32)
    out_ref[...] = buf[:total, :].astype(BF16)


def attend_kernel(before_ref, role_ref, scale_ref, x0, x1, x2, x3, out_ref, ds_ref, arr, res):
    shards, slots, hdim = out_ref.shape
    total = x0.shape[0]
    blk = 256
    inv = 1.0 / math.sqrt(hdim)
    role = role_ref[0]
    scale = scale_ref[0]
    coef = scale * inv
    for i, ref in enumerate((x0, x1, x2, x3)):
        arr[role ^ i] = ref[...]
    res[...] = jnp.zeros_like(res)
    q_ref, k_ref, v_ref, g_ref = (arr.at[i] for i in range(PARTS))
    kt = k_ref[...].astype(F32).T.astype(BF16)
    vt = v_ref[...].astype(F32).T.astype(BF16)
    tri = lax.broadcasted_iota(jnp.int32, (blk, blk), 0) <= lax.broadcasted_iota(
        jnp.int32, (blk, blk), 1
    )
    dsc = jnp.zeros((1, blk), F32)
    for lo in range(0, total, blk):
        n = lo + blk
        qi = q_ref[lo:n, :]
        gi = g_ref[lo:n, :]
        raw = lax.dot_general(k_ref[:n, :], qi, NT, preferred_element_type=F32)
        s = raw * coef
        diag = jnp.where(tri, s[lo:, :], -jnp.inf)
        top = jnp.max(diag, axis=0, keepdims=True)
        if lo:
            top = jnp.maximum(top, jnp.max(s[:lo, :], axis=0, keepdims=True))
            s = jnp.concatenate([s[:lo, :], diag], axis=0)
        else:
            s = diag
        e = jnp.exp(s - top)
        p = e * (1.0 / jnp.sum(e, axis=0, keepdims=True))
        pb = p.astype(BF16)
        att = jnp.dot(vt[:, :n], pb, preferred_element_type=F32).astype(BF16)
        git = gi.astype(F32).T
        delta = jnp.sum(git * att.astype(F32), axis=0, keepdims=True)
        dp = lax.dot_general(v_ref[:n, :], gi, NT, preferred_element_type=F32)
        ds = p * (dp - delta)
        dsc = dsc + jnp.sum(ds * raw, axis=0, keepdims=True)
        dsb = ds.astype(BF16)

        @pl.when(role == 0)
        def _():
            res[lo:n, :] = att.astype(F32).T

        @pl.when(role == 1)
        def _():
            res[lo:n, :] = coef * jnp.dot(kt[:, :n], dsb, preferred_element_type=F32).T

        @pl.when(role == 2)
        def _():
            res[:n, :] += coef * jnp.dot(dsb, qi, preferred_element_type=F32)

        @pl.when(role == 3)
        def _():
            res[:n, :] += jnp.dot(pb, gi, preferred_element_type=F32)

    ds_ref[...] = jnp.broadcast_to(jnp.sum(dsc, axis=1, keepdims=True) * inv, ds_ref.shape)
    for c in range(shards):
        out_ref[c] = res[pl.ds(before_ref[c], slots), :].astype(BF16)


def place_kernel(
    here_ref, places_ref, logit_ref, g_ref, in_ref, bo_ref, dq_ref, dk_ref, dv_ref, dl_ref
):
    tok, width = g_ref.shape
    slots, hdim = in_ref.shape[1:]
    col = slot_column(places_ref[...], here_ref[0] * tok, tok)
    hit = lax.broadcasted_iota(jnp.int32, (tok, slots), 1).astype(F32) + 1.0 == col
    spread = hit.astype(BF16)
    gate_row = sigmoid(logit_ref[...])
    gate = to_col(gate_row, tok)
    acc = jnp.zeros((tok, hdim), F32)
    for head in range(width // hdim):
        cols = slice(head * hdim, (head + 1) * hdim)
        att = jnp.dot(spread, in_ref[head * PARTS], preferred_element_type=F32)
        bo_ref[:, cols] = (gate * att).astype(BF16)
        acc = acc + g_ref[:, cols].astype(F32) * att
        for part, ref in ((1, dq_ref), (2, dk_ref), (3, dv_ref)):
            ref[:, cols] = jnp.dot(
                spread, in_ref[head * PARTS + part], preferred_element_type=F32
            ).astype(BF16)
    dot = to_row(jnp.sum(acc, axis=1, keepdims=True), tok)
    dl_ref[...] = gate_row * (1.0 - gate_row) * dot


def body(queries, keys, values, router_logit, head_scale, routed, grad_out):
    nctx = lax.axis_size("ctx")
    here = lax.axis_index("ctx")
    tok, width = queries.shape[1:]
    heads = head_scale.shape[0]
    hdim = width // heads
    total = routed.shape[1]
    rows = total // nctx
    slots = rows + 3 * (rows // 2)
    here_vec = here.astype(jnp.int32)[None]
    role = (here % PARTS).astype(jnp.int32)[None]
    head = here // PARTS
    scale = lax.dynamic_slice_in_dim(head_scale, head, 1)
    starts = jnp.arange(nctx, dtype=jnp.int32) * tok
    before = jnp.sum((routed[0][None, :] < starts[:, None]).astype(jnp.int32), axis=1)
    params = pltpu.CompilerParams(vmem_limit_bytes=48 * 1024 * 1024)

    send = pl.pallas_call(
        pack_kernel,
        out_shape=jax.ShapeDtypeStruct((nctx, slots, hdim), BF16),
        in_specs=[SM] + [VM] * 6,
        out_specs=VM,
        compiler_params=params,
        name="pack",
    )(here_vec, routed, router_logit, queries[0], keys[0], values[0], grad_out[0])
    got = lax.all_to_all(send, "ctx", split_axis=0, concat_axis=0, tiled=True)
    own = pl.pallas_call(
        compact_kernel,
        out_shape=jax.ShapeDtypeStruct((total, hdim), BF16),
        in_specs=[SM, VM],
        out_specs=VM,
        scratch_shapes=[pltpu.VMEM((total + slots, hdim), F32)],
        compiler_params=params,
        name="compact",
    )(before, got)
    side = lax.ppermute(own, "ctx", [(i, i ^ 2) for i in range(nctx)])
    near = lax.ppermute(own, "ctx", [(i, i ^ 1) for i in range(nctx)])
    cross = lax.ppermute(side, "ctx", [(i, i ^ 1) for i in range(nctx)])
    back, dsc = pl.pallas_call(
        attend_kernel,
        out_shape=(
            jax.ShapeDtypeStruct((nctx, slots, hdim), BF16),
            jax.ShapeDtypeStruct((8, 128), F32),
        ),
        in_specs=[SM] * 3 + [VM] * 4,
        out_specs=(VM, VM),
        scratch_shapes=[
            pltpu.VMEM((PARTS, total, hdim), BF16),
            pltpu.VMEM((total + slots, hdim), F32),
        ],
        compiler_params=params,
        name="attend",
    )(before, role, scale, own, near, side, cross)
    home = lax.all_to_all(back, "ctx", split_axis=0, concat_axis=0, tiled=True)
    dsc = lax.psum(dsc, "dp")
    groups = [[PARTS * i + j for i in range(heads)] for j in range(nctx // heads)]
    all_dsc = lax.all_to_all(
        jnp.broadcast_to(dsc[None], (heads,) + dsc.shape),
        "ctx",
        split_axis=0,
        concat_axis=0,
        axis_index_groups=groups,
        tiled=True,
    )
    outs = pl.pallas_call(
        place_kernel,
        out_shape=tuple([jax.ShapeDtypeStruct((tok, width), BF16)] * 4)
        + (jax.ShapeDtypeStruct((1, tok), F32),),
        in_specs=[SM] + [VM] * 4,
        out_specs=(VM,) * 5,
        compiler_params=params,
        name="place",
    )(here_vec, routed, router_logit, grad_out[0], home)
    block_out, d_q, d_k, d_v, d_logit = outs
    return block_out[None], d_q[None], d_k[None], d_v[None], d_logit, all_dsc[:, 0, 0]


def solution(mesh):
    in_specs = (
        P("dp", "ctx", None),
        P("dp", "ctx", None),
        P("dp", "ctx", None),
        P("dp", "ctx"),
        P(),
        P("dp", None),
        P("dp", "ctx", None),
    )
    out_specs = (
        P("dp", "ctx", None),
        P("dp", "ctx", None),
        P("dp", "ctx", None),
        P("dp", "ctx", None),
        P("dp", "ctx"),
        P(),
    )
    return jax.shard_map(body, mesh=mesh, in_specs=in_specs, out_specs=out_specs, check_vma=False)
```

```python
import functools
import math

import jax
import jax.numpy as jnp
from jax import lax
from jax.experimental import pallas as pl
from jax.experimental.pallas import tpu as pltpu
from jax.sharding import PartitionSpec as P

F32 = jnp.float32
BF16 = jnp.bfloat16
VM = pl.BlockSpec(memory_space=pltpu.VMEM)
SM = pl.BlockSpec(memory_space=pltpu.SMEM)
HB = pl.BlockSpec(memory_space=pltpu.HBM)
NT = (((1,), (1,)), ((), ()))
PARTS = 4


def eye(n):
    return lax.broadcasted_iota(jnp.int32, (n, n), 0) == lax.broadcasted_iota(jnp.int32, (n, n), 1)


def to_row(col, n):
    return jnp.sum(jnp.where(eye(n), col, 0.0), axis=0, keepdims=True)


def to_col(row, n):
    return jnp.sum(jnp.where(eye(n), row, 0.0), axis=1, keepdims=True)


def slot_column(places, first, tok):
    total = places.shape[1]
    before = jnp.sum((places < first).astype(F32), axis=1, keepdims=True)
    rank = lax.broadcasted_iota(jnp.int32, (1, total), 1).astype(F32) + 1.0 - before
    here = places - first == lax.broadcasted_iota(jnp.int32, (tok, total), 0)
    return jnp.sum(jnp.where(here, rank, 0.0), axis=1, keepdims=True)


def sigmoid(x):
    return 1.0 / (1.0 + jnp.exp(-x))


def pack_kernel(here_ref, places_ref, logit_ref, q_ref, k_ref, v_ref, g_ref, out_ref, buf, sems):
    tok, width = q_ref.shape
    slots, hdim = out_ref.shape[1:]
    copies = [
        pltpu.make_async_copy(ref, buf.at[part], sems.at[part])
        for part, ref in enumerate((q_ref, k_ref, v_ref, g_ref))
    ]
    for copy in copies:
        copy.start()
    row = to_row(slot_column(places_ref[...], here_ref[0] * tok, tok), tok)
    hit = lax.broadcasted_iota(jnp.int32, (slots, tok), 0).astype(F32) + 1.0 == row
    pick = hit.astype(BF16)
    gate = jnp.sum(jnp.where(hit, sigmoid(logit_ref[...]), 0.0), axis=1, keepdims=True)
    for part, copy in enumerate(copies):
        copy.wait()
        for base in range(0, width, 4 * hdim):
            rows = jnp.dot(pick, buf[part, :, base : base + 4 * hdim], preferred_element_type=F32)
            if part == 3:
                rows = rows * gate
            rows = rows.astype(BF16)
            for i in range(4):
                head = base // hdim + i
                out_ref[head * PARTS + part] = rows[:, i * hdim : (i + 1) * hdim]


def compact_kernel(before_ref, in_ref, out_ref, buf):
    shards, slots, _ = in_ref.shape
    total = out_ref.shape[0]
    for c in range(shards):
        buf[pl.ds(before_ref[c], slots), :] = in_ref[c].astype(F32)
    out_ref[...] = buf[:total, :].astype(BF16)


def fold(x, op):
    return op(x.reshape(x.shape[0] // 8, 8, x.shape[1]), axis=0)


def attend_kernel(
    before_ref, role_ref, head_ref, scale_ref, x0, x1, x2, x3, out_ref, ds_ref, arr, res, pbuf, dbuf, abuf, rbuf, gbuf
):
    shards, slots, hdim = out_ref.shape
    total = x0.shape[0]
    blk = 256
    strip = 32
    inv = 1.0 / math.sqrt(hdim)
    role = role_ref[0]
    scale = scale_ref[0]
    coef = scale * inv
    coef2 = coef * math.log2(math.e)
    for i, ref in enumerate((x0, x1, x2, x3)):
        arr[role ^ i] = ref[...]
    q_ref, k_ref, v_ref, g_ref = (arr.at[i] for i in range(PARTS))
    blocks = range(0, total, blk)

    def scores(lo):
        n = lo + blk
        raw = lax.dot_general(k_ref[:n, :], q_ref[lo:n, :], NT, preferred_element_type=F32)
        rbuf[:n, lo:n] = raw

    def products(lo):
        n = lo + blk
        gbuf[:n, lo:n] = lax.dot_general(
            v_ref[:n, :], g_ref[lo:n, :], NT, preferred_element_type=F32
        )

    def strips(lo):
        return [(a, slice(a, a + strip)) for a in range(0, lo + blk, strip)]

    def masked(x, a, lo):
        if a + strip <= lo:
            return x
        row = lax.broadcasted_iota(jnp.int32, (strip, blk), 0) + (a - lo)
        return jnp.where(row <= lax.broadcasted_iota(jnp.int32, (strip, blk), 1), x, -jnp.inf)

    scores(0)
    products(0)
    vt = v_ref[...].astype(F32).T.astype(BF16)
    dsc = jnp.zeros((8, blk), F32)
    for lo in blocks:
        n = lo + blk
        cols = slice(lo, n)
        if n < total:
            scores(n)
        top = jnp.full((8, blk), -jnp.inf, F32)
        for a, rows in strips(lo):
            top = jnp.maximum(top, fold(masked(rbuf[rows, cols], a, lo), jnp.max))
        top = jnp.max(top, axis=0, keepdims=True) * coef2
        acc = jnp.zeros((8, blk), F32)
        for a, rows in strips(lo):
            acc = acc + fold(jnp.exp2(masked(rbuf[rows, cols], a, lo) * coef2 - top), jnp.sum)
        lse = top + jnp.log2(jnp.sum(acc, axis=0, keepdims=True))
        for a, rows in strips(lo):
            p = jnp.exp2(masked(rbuf[rows, cols], a, lo) * coef2 - lse)
            pbuf[rows, cols] = p.astype(BF16)
        att = jnp.dot(vt[:, :n], pbuf[:n, cols], preferred_element_type=F32).astype(BF16)
        abuf[:, cols] = att
        if n < total:
            products(n)
        git = g_ref[lo:n, :].astype(F32).T
        delta = jnp.sum(git * att.astype(F32), axis=0, keepdims=True)
        for a, rows in strips(lo):
            raw = rbuf[rows, cols]
            ds = jnp.exp2(masked(raw, a, lo) * coef2 - lse) * (gbuf[rows, cols] - delta)
            dsc = dsc + fold(ds * raw, jnp.sum)
            dbuf[rows, cols] = ds.astype(BF16)
    mine = lax.broadcasted_iota(jnp.int32, ds_ref.shape, 1) == head_ref[0]
    dsum = jnp.sum(jnp.sum(dsc, axis=0, keepdims=True), axis=1, keepdims=True)
    ds_ref[...] = jnp.where(mine, dsum * inv, 0.0)

    @pl.when(role == 0)
    def _():
        res[:total, :] = abuf[...].astype(F32).T

    @pl.when(role == 1)
    def _():
        kt = k_ref[...].astype(F32).T.astype(BF16)
        for lo in blocks:
            n = lo + blk
            dq = jnp.dot(kt[:, :n], dbuf[:n, lo:n], preferred_element_type=F32)
            res[lo:n, :] = (coef * dq).T

    @pl.when(role == 2)
    def _():
        for lo in blocks:
            res[lo : lo + blk, :] = coef * jnp.dot(
                dbuf[lo : lo + blk, lo:], q_ref[lo:, :], preferred_element_type=F32
            )

    @pl.when(role == 3)
    def _():
        for lo in blocks:
            res[lo : lo + blk, :] = jnp.dot(
                pbuf[lo : lo + blk, lo:], g_ref[lo:, :], preferred_element_type=F32
            )

    res[total:, :] = jnp.zeros((slots, hdim), F32)
    for c in range(shards):
        out_ref[c] = res[pl.ds(before_ref[c], slots), :].astype(BF16)


def place_kernel(
    here_ref, places_ref, logit_ref, g_ref, in_ref, bo_ref, dq_ref, dk_ref, dv_ref, dl_ref
):
    tok, width = g_ref.shape
    slots, hdim = in_ref.shape[1:]
    col = slot_column(places_ref[...], here_ref[0] * tok, tok)
    hit = lax.broadcasted_iota(jnp.int32, (tok, slots), 1).astype(F32) + 1.0 == col
    spread = hit.astype(BF16)
    gate_row = sigmoid(logit_ref[...])
    gate = to_col(gate_row, tok)
    acc = jnp.zeros((tok, hdim), F32)
    for head in range(width // hdim):
        cols = slice(head * hdim, (head + 1) * hdim)
        att = jnp.dot(spread, in_ref[head * PARTS], preferred_element_type=F32)
        bo_ref[:, cols] = (gate * att).astype(BF16)
        acc = acc + g_ref[:, cols].astype(F32) * att
        for part, ref in ((1, dq_ref), (2, dk_ref), (3, dv_ref)):
            ref[:, cols] = jnp.dot(
                spread, in_ref[head * PARTS + part], preferred_element_type=F32
            ).astype(BF16)
    dot = to_row(jnp.sum(acc, axis=1, keepdims=True), tok)
    dl_ref[...] = gate_row * (1.0 - gate_row) * dot


def body(queries, keys, values, router_logit, head_scale, routed, grad_out):
    nctx = lax.axis_size("ctx")
    here = lax.axis_index("ctx")
    tok, width = queries.shape[1:]
    heads = head_scale.shape[0]
    hdim = width // heads
    total = routed.shape[1]
    rows = total // nctx
    slots = rows + 3 * (rows // 2)
    here_vec = here.astype(jnp.int32)[None]
    role = (here % PARTS).astype(jnp.int32)[None]
    head = (here // PARTS).astype(jnp.int32)
    scale = lax.dynamic_slice_in_dim(head_scale, head, 1)
    starts = jnp.arange(nctx, dtype=jnp.int32) * tok
    before = jnp.sum((routed[0][None, :] < starts[:, None]).astype(jnp.int32), axis=1)
    params = pltpu.CompilerParams(vmem_limit_bytes=48 * 1024 * 1024)

    send = pl.pallas_call(
        pack_kernel,
        out_shape=jax.ShapeDtypeStruct((nctx, slots, hdim), BF16),
        in_specs=[SM] + [VM] * 2 + [HB] * 4,
        out_specs=VM,
        scratch_shapes=[pltpu.VMEM((PARTS, tok, width), BF16), pltpu.SemaphoreType.DMA((PARTS,))],
        compiler_params=pltpu.CompilerParams(vmem_limit_bytes=60 * 1024 * 1024),
        name="pack",
    )(here_vec, routed, router_logit, queries[0], keys[0], values[0], grad_out[0])
    got = lax.all_to_all(send, "ctx", split_axis=0, concat_axis=0, tiled=True)
    own = pl.pallas_call(
        compact_kernel,
        out_shape=jax.ShapeDtypeStruct((total, hdim), BF16),
        in_specs=[SM, VM],
        out_specs=VM,
        scratch_shapes=[pltpu.VMEM((total + slots, hdim), F32)],
        compiler_params=params,
        name="compact",
    )(before, got)
    side = lax.ppermute(own, "ctx", [(i, i ^ 2) for i in range(nctx)])
    near = lax.ppermute(own, "ctx", [(i, i ^ 1) for i in range(nctx)])
    cross = lax.ppermute(side, "ctx", [(i, i ^ 1) for i in range(nctx)])
    back, dsc = pl.pallas_call(
        attend_kernel,
        out_shape=(
            jax.ShapeDtypeStruct((nctx, slots, hdim), BF16),
            jax.ShapeDtypeStruct((1, 128), F32),
        ),
        in_specs=[SM] * 4 + [VM] * 4,
        out_specs=(VM, VM),
        scratch_shapes=[
            pltpu.VMEM((PARTS, total, hdim), BF16),
            pltpu.VMEM((total + slots, hdim), F32),
            pltpu.VMEM((total, total), BF16),
            pltpu.VMEM((total, total), BF16),
            pltpu.VMEM((hdim, total), BF16),
            pltpu.VMEM((total, total), F32),
            pltpu.VMEM((total, total), F32),
        ],
        compiler_params=params,
        name="attend",
    )(before, role, head[None], scale, own, near, side, cross)
    home = lax.all_to_all(back, "ctx", split_axis=0, concat_axis=0, tiled=True)
    dsc = lax.psum(dsc, "dp")
    home, dsc = lax.optimization_barrier((home, dsc))
    groups = [[PARTS * i + j for i in range(heads)] for j in range(nctx // heads)]
    dsc = lax.all_to_all(
        jnp.broadcast_to(dsc[None], (heads,) + dsc.shape),
        "ctx",
        split_axis=0,
        concat_axis=0,
        axis_index_groups=groups,
        tiled=True,
    )
    outs = pl.pallas_call(
        place_kernel,
        out_shape=tuple([jax.ShapeDtypeStruct((tok, width), BF16)] * 4)
        + (jax.ShapeDtypeStruct((1, tok), F32),),
        in_specs=[SM] + [VM] * 4,
        out_specs=(VM,) * 5,
        compiler_params=params,
        name="place",
    )(here_vec, routed, router_logit, grad_out[0], home)
    block_out, d_q, d_k, d_v, d_logit = outs
    return block_out[None], d_q[None], d_k[None], d_v[None], d_logit, jnp.sum(dsc[:, 0, :heads], axis=0)


def solution(mesh):
    in_specs = (
        P("dp", "ctx", None),
        P("dp", "ctx", None),
        P("dp", "ctx", None),
        P("dp", "ctx"),
        P(),
        P("dp", None),
        P("dp", "ctx", None),
    )
    out_specs = (
        P("dp", "ctx", None),
        P("dp", "ctx", None),
        P("dp", "ctx", None),
        P("dp", "ctx", None),
        P("dp", "ctx"),
        P(),
    )
    return jax.shard_map(body, mesh=mesh, in_specs=in_specs, out_specs=out_specs, check_vma=False)
```

```python
import functools
import math

import jax
import jax.numpy as jnp
from jax import lax
from jax.experimental import pallas as pl
from jax.experimental.pallas import tpu as pltpu
from jax.sharding import PartitionSpec as P

F32 = jnp.float32
BF16 = jnp.bfloat16
VM = pl.BlockSpec(memory_space=pltpu.VMEM)
SM = pl.BlockSpec(memory_space=pltpu.SMEM)
HB = pl.BlockSpec(memory_space=pltpu.HBM)
NT = (((1,), (1,)), ((), ()))
PARTS = 4


def eye(n):
    return lax.broadcasted_iota(jnp.int32, (n, n), 0) == lax.broadcasted_iota(jnp.int32, (n, n), 1)


def to_row(col, n):
    return jnp.sum(jnp.where(eye(n), col, 0.0), axis=0, keepdims=True)


def to_col(row, n):
    return jnp.sum(jnp.where(eye(n), row, 0.0), axis=1, keepdims=True)


def slot_column(places, first, tok):
    total = places.shape[1]
    before = jnp.sum((places < first).astype(F32), axis=1, keepdims=True)
    rank = lax.broadcasted_iota(jnp.int32, (1, total), 1).astype(F32) + 1.0 - before
    here = places - first == lax.broadcasted_iota(jnp.int32, (tok, total), 0)
    return jnp.sum(jnp.where(here, rank, 0.0), axis=1, keepdims=True)


def sigmoid(x):
    return 1.0 / (1.0 + jnp.exp(-x))


def pack_kernel(
    here_ref, places_hbm, logit_hbm, q_hbm, k_hbm, v_hbm, g_hbm, out_hbm, places, logit, buf, out, sems, out_sems
):
    tok, width = q_hbm.shape
    heads, _, slots, hdim = out.shape
    small = [
        pltpu.make_async_copy(src, dst, sems.at[PARTS + i])
        for i, (src, dst) in enumerate(((places_hbm, places), (logit_hbm, logit)))
    ]
    copies = [
        pltpu.make_async_copy(ref, buf.at[part], sems.at[part])
        for part, ref in enumerate((q_hbm, k_hbm, v_hbm, g_hbm))
    ]
    for copy in small + copies:
        copy.start()
    for copy in small:
        copy.wait()
    row = to_row(slot_column(places[...], here_ref[0] * tok, tok), tok)
    hit = lax.broadcasted_iota(jnp.int32, (slots, tok), 0).astype(F32) + 1.0 == row
    pick = hit.astype(BF16)
    gate = jnp.sum(jnp.where(hit, sigmoid(logit[...]), 0.0), axis=1, keepdims=True)
    sends = []
    for part, copy in enumerate(copies):
        copy.wait()
        for base in range(0, width, 4 * hdim):
            rows = jnp.dot(pick, buf[part, :, base : base + 4 * hdim], preferred_element_type=F32)
            if part == 3:
                rows = rows * gate
            rows = rows.astype(BF16)
            for i in range(4):
                out[base // hdim + i, part] = rows[:, i * hdim : (i + 1) * hdim]
        send = pltpu.make_async_copy(out.at[:, part], out_hbm.at[:, part], out_sems.at[part])
        send.start()
        sends.append(send)
    for send in sends:
        send.wait()


def compact_kernel(before_ref, in_ref, out_ref, buf):
    shards, slots, _ = in_ref.shape
    total = out_ref.shape[0]
    for c in range(shards):
        buf[pl.ds(before_ref[c], slots), :] = in_ref[c].astype(F32)
    out_ref[...] = buf[:total, :].astype(BF16)


def fold(x, op):
    return op(x.reshape(x.shape[0] // 8, 8, x.shape[1]), axis=0)


def attend_kernel(
    before_ref, here_ref, scale_ref, x0, x1, x2, x3, out_ref, ds_ref, arr, res, pbuf, dbuf, abuf, rbuf, gbuf
):
    shards, slots, hdim = out_ref.shape
    total = x0.shape[0]
    blk = 256
    strip = 32
    inv = 1.0 / math.sqrt(hdim)
    role = lax.rem(here_ref[0], PARTS)
    head = lax.div(here_ref[0], PARTS)
    coef = scale_ref[head] * inv
    coef2 = coef * math.log2(math.e)
    for i, ref in enumerate((x0, x1, x2, x3)):
        arr[role ^ i] = ref[...]
    q_ref, k_ref, v_ref, g_ref = (arr.at[i] for i in range(PARTS))
    blocks = range(0, total, blk)

    def scores(lo):
        n = lo + blk
        raw = lax.dot_general(k_ref[:n, :], q_ref[lo:n, :], NT, preferred_element_type=F32)
        rbuf[:n, lo:n] = raw

    def products(lo):
        n = lo + blk
        gbuf[:n, lo:n] = lax.dot_general(
            v_ref[:n, :], g_ref[lo:n, :], NT, preferred_element_type=F32
        )

    def strips(lo):
        return [(a, slice(a, a + strip)) for a in range(0, lo + blk, strip)]

    def masked(x, a, lo):
        if a + strip <= lo:
            return x
        row = lax.broadcasted_iota(jnp.int32, (strip, blk), 0) + (a - lo)
        return jnp.where(row <= lax.broadcasted_iota(jnp.int32, (strip, blk), 1), x, -jnp.inf)

    def softmax(lo):
        cols = slice(lo, lo + blk)
        top = jnp.full((8, blk), -jnp.inf, F32)
        for a, rows in strips(lo):
            top = jnp.maximum(top, fold(masked(rbuf[rows, cols], a, lo), jnp.max))
        top = jnp.max(top, axis=0, keepdims=True) * coef2
        acc = jnp.zeros((8, blk), F32)
        for a, rows in strips(lo):
            acc = acc + fold(jnp.exp2(masked(rbuf[rows, cols], a, lo) * coef2 - top), jnp.sum)
        lse = top + jnp.log2(jnp.sum(acc, axis=0, keepdims=True))
        for a, rows in strips(lo):
            p = jnp.exp2(masked(rbuf[rows, cols], a, lo) * coef2 - lse)
            pbuf[rows, cols] = p.astype(BF16)
        return lse

    def attended(lo):
        n = lo + blk
        att = jnp.dot(vt[:, :n], pbuf[:n, lo:n], preferred_element_type=F32).astype(BF16)
        abuf[:, lo:n] = att
        git = g_ref[lo:n, :].astype(F32).T
        return jnp.sum(git * att.astype(F32), axis=0, keepdims=True)

    def backward(lo, lse, delta, dsc):
        cols = slice(lo, lo + blk)
        for a, rows in strips(lo):
            raw = rbuf[rows, cols]
            ds = jnp.exp2(masked(raw, a, lo) * coef2 - lse) * (gbuf[rows, cols] - delta)
            dsc = dsc + fold(ds * raw, jnp.sum)
            dbuf[rows, cols] = ds.astype(BF16)
        return dsc

    vt = v_ref[...].astype(F32).T.astype(BF16)
    dsc = jnp.zeros((8, blk), F32)
    for lo in blocks:
        scores(lo)
    lses = []
    for lo in blocks:
        lses.append(softmax(lo))
        products(lo)
    deltas = [attended(lo) for lo in blocks]
    for lo, lse, delta in zip(blocks, lses, deltas):
        dsc = backward(lo, lse, delta, dsc)
    mine = lax.broadcasted_iota(jnp.int32, ds_ref.shape, 1) == head
    dsum = jnp.sum(jnp.sum(dsc, axis=0, keepdims=True), axis=1, keepdims=True)
    ds_ref[...] = jnp.where(mine, dsum * inv, 0.0)

    @pl.when(role == 0)
    def _():
        res[:total, :] = abuf[...].astype(F32).T

    @pl.when(role == 1)
    def _():
        kt = k_ref[...].astype(F32).T.astype(BF16)
        for lo in blocks:
            n = lo + blk
            dq = jnp.dot(kt[:, :n], dbuf[:n, lo:n], preferred_element_type=F32)
            res[lo:n, :] = (coef * dq).T

    @pl.when(role == 2)
    def _():
        for lo in blocks:
            res[lo : lo + blk, :] = coef * jnp.dot(
                dbuf[lo : lo + blk, lo:], q_ref[lo:, :], preferred_element_type=F32
            )

    @pl.when(role == 3)
    def _():
        for lo in blocks:
            res[lo : lo + blk, :] = jnp.dot(
                pbuf[lo : lo + blk, lo:], g_ref[lo:, :], preferred_element_type=F32
            )

    res[total:, :] = jnp.zeros((slots, hdim), F32)
    for c in range(shards):
        out_ref[c] = res[pl.ds(before_ref[c], slots), :].astype(BF16)


def place_kernel(
    here_ref, places_ref, logit_ref, g_ref, in_ref, bo_ref, dq_ref, dk_ref, dv_ref, dl_ref
):
    tok, width = g_ref.shape
    slots, hdim = in_ref.shape[1:]
    col = slot_column(places_ref[...], here_ref[0] * tok, tok)
    hit = lax.broadcasted_iota(jnp.int32, (tok, slots), 1).astype(F32) + 1.0 == col
    spread = hit.astype(BF16)
    gate_row = sigmoid(logit_ref[...])
    gate = to_col(gate_row, tok)
    acc = jnp.zeros((tok, 2 * hdim), F32)
    for head in range(0, width // hdim, 2):
        cols = slice(head * hdim, (head + 2) * hdim)

        def home(part):
            pair = [in_ref[(head + i) * PARTS + part] for i in range(2)]
            return jnp.dot(spread, jnp.concatenate(pair, axis=1), preferred_element_type=F32)

        att = home(0)
        bo_ref[:, cols] = (gate * att).astype(BF16)
        acc = acc + g_ref[:, cols].astype(F32) * att
        dq_ref[:, cols] = home(1).astype(BF16)
        dk_ref[:, cols] = home(2).astype(BF16)
        dv_ref[:, cols] = home(3).astype(BF16)
    dot = to_row(jnp.sum(acc, axis=1, keepdims=True), tok)
    dl_ref[...] = gate_row * (1.0 - gate_row) * dot


def body(queries, keys, values, router_logit, head_scale, routed, grad_out):
    nctx = lax.axis_size("ctx")
    here = lax.axis_index("ctx")
    tok, width = queries.shape[1:]
    heads = head_scale.shape[0]
    hdim = width // heads
    total = routed.shape[1]
    rows = total // nctx
    slots = rows + 3 * (rows // 2)
    here_vec = here.astype(jnp.int32)[None]
    starts = jnp.arange(nctx, dtype=jnp.int32) * tok
    before = jnp.sum((routed[0][None, :] < starts[:, None]).astype(jnp.int32), axis=1)
    params = pltpu.CompilerParams(vmem_limit_bytes=48 * 1024 * 1024)

    send = pl.pallas_call(
        pack_kernel,
        out_shape=jax.ShapeDtypeStruct((heads, PARTS, slots, hdim), BF16),
        in_specs=[SM] + [HB] * 6,
        out_specs=HB,
        scratch_shapes=[
            pltpu.VMEM((1, total), jnp.int32),
            pltpu.VMEM((1, tok), F32),
            pltpu.VMEM((PARTS, tok, width), BF16),
            pltpu.VMEM((heads, PARTS, slots, hdim), BF16),
            pltpu.SemaphoreType.DMA((PARTS + 2,)),
            pltpu.SemaphoreType.DMA((PARTS,)),
        ],
        compiler_params=pltpu.CompilerParams(vmem_limit_bytes=60 * 1024 * 1024),
        name="pack",
    )(here_vec, routed, router_logit, queries[0], keys[0], values[0], grad_out[0])
    send = send.reshape(nctx, slots, hdim)
    got = lax.all_to_all(send, "ctx", split_axis=0, concat_axis=0, tiled=True)
    own = pl.pallas_call(
        compact_kernel,
        out_shape=jax.ShapeDtypeStruct((total, hdim), BF16),
        in_specs=[SM, VM],
        out_specs=VM,
        scratch_shapes=[pltpu.VMEM((total + slots, hdim), F32)],
        compiler_params=params,
        name="compact",
    )(before, got)
    side = lax.ppermute(own, "ctx", [(i, i ^ 2) for i in range(nctx)])
    near = lax.ppermute(own, "ctx", [(i, i ^ 1) for i in range(nctx)])
    cross = lax.ppermute(side, "ctx", [(i, i ^ 1) for i in range(nctx)])
    back, dsc = pl.pallas_call(
        attend_kernel,
        out_shape=(
            jax.ShapeDtypeStruct((nctx, slots, hdim), BF16),
            jax.ShapeDtypeStruct((1, 128), F32),
        ),
        in_specs=[SM] * 3 + [VM] * 4,
        out_specs=(VM, VM),
        scratch_shapes=[
            pltpu.VMEM((PARTS, total, hdim), BF16),
            pltpu.VMEM((total + slots, hdim), F32),
            pltpu.VMEM((total, total), BF16),
            pltpu.VMEM((total, total), BF16),
            pltpu.VMEM((hdim, total), BF16),
            pltpu.VMEM((total, total), F32),
            pltpu.VMEM((total, total), F32),
        ],
        compiler_params=params,
        name="attend",
    )(before, here_vec, head_scale, own, near, side, cross)
    groups = [[PARTS * i + j for i in range(heads)] for j in range(nctx // heads)]
    dsc = lax.all_to_all(
        jnp.broadcast_to(dsc[None], (heads,) + dsc.shape),
        "ctx",
        split_axis=0,
        concat_axis=0,
        axis_index_groups=groups,
        tiled=True,
    )
    back, dsc = lax.optimization_barrier((back, dsc))
    home = lax.all_to_all(back, "ctx", split_axis=0, concat_axis=0, tiled=True)
    dsc = lax.psum(jnp.sum(dsc, axis=0)[:, :heads], "dp")
    home, dsc = lax.optimization_barrier((home, dsc))
    outs = pl.pallas_call(
        place_kernel,
        out_shape=tuple([jax.ShapeDtypeStruct((tok, width), BF16)] * 4)
        + (jax.ShapeDtypeStruct((1, tok), F32),),
        in_specs=[SM] + [VM] * 4,
        out_specs=(VM,) * 5,
        compiler_params=params,
        name="place",
    )(here_vec, routed, router_logit, grad_out[0], home)
    block_out, d_q, d_k, d_v, d_logit = outs
    return block_out[None], d_q[None], d_k[None], d_v[None], d_logit, dsc[0]


def solution(mesh):
    in_specs = (
        P("dp", "ctx", None),
        P("dp", "ctx", None),
        P("dp", "ctx", None),
        P("dp", "ctx"),
        P(),
        P("dp", None),
        P("dp", "ctx", None),
    )
    out_specs = (
        P("dp", "ctx", None),
        P("dp", "ctx", None),
        P("dp", "ctx", None),
        P("dp", "ctx", None),
        P("dp", "ctx"),
        P(),
    )
    return jax.shard_map(body, mesh=mesh, in_specs=in_specs, out_specs=out_specs, check_vma=False)
```

```python
import functools
import math

import jax
import jax.numpy as jnp
from jax import lax
from jax.experimental import pallas as pl
from jax.experimental.pallas import tpu as pltpu
from jax.sharding import PartitionSpec as P

F32 = jnp.float32
BF16 = jnp.bfloat16
VM = pl.BlockSpec(memory_space=pltpu.VMEM)
SM = pl.BlockSpec(memory_space=pltpu.SMEM)
HB = pl.BlockSpec(memory_space=pltpu.HBM)
NT = (((1,), (1,)), ((), ()))
PARTS = 4
FAR = -3e38
BLK = 256
STRIP = 32


def eye(n):
    return lax.broadcasted_iota(jnp.int32, (n, n), 0) == lax.broadcasted_iota(jnp.int32, (n, n), 1)


def to_row(col, n):
    return jnp.sum(jnp.where(eye(n), col, 0.0), axis=0, keepdims=True)


def to_col(row, n):
    return jnp.sum(jnp.where(eye(n), row, 0.0), axis=1, keepdims=True)


def slot_column(places, first, tok):
    total = places.shape[1]
    before = jnp.sum((places < first).astype(F32), axis=1, keepdims=True)
    rank = lax.broadcasted_iota(jnp.int32, (1, total), 1).astype(F32) + 1.0 - before
    here = places - first == lax.broadcasted_iota(jnp.int32, (tok, total), 0)
    return jnp.sum(jnp.where(here, rank, 0.0), axis=1, keepdims=True)


def sigmoid(x):
    return 1.0 / (1.0 + jnp.exp(-x))


def pack_kernel(
    here_ref, places_hbm, logit_hbm, q_hbm, k_hbm, v_hbm, g_hbm, out_hbm, places, logit, buf, out, sems, out_sems
):
    tok, width = q_hbm.shape
    heads, _, slots, hdim = out.shape
    small = [
        pltpu.make_async_copy(src, dst, sems.at[PARTS + i])
        for i, (src, dst) in enumerate(((places_hbm, places), (logit_hbm, logit)))
    ]
    copies = [
        pltpu.make_async_copy(ref, buf.at[part], sems.at[part])
        for part, ref in enumerate((q_hbm, k_hbm, v_hbm, g_hbm))
    ]
    for copy in small + copies:
        copy.start()
    for copy in small:
        copy.wait()
    row = to_row(slot_column(places[...], here_ref[0] * tok, tok), tok)
    hit = lax.broadcasted_iota(jnp.int32, (slots, tok), 0).astype(F32) + 1.0 == row
    pick = hit.astype(BF16)
    gate = jnp.sum(jnp.where(hit, sigmoid(logit[...]), 0.0), axis=1, keepdims=True)
    sends = []
    for part, copy in enumerate(copies):
        copy.wait()
        for base in range(0, width, 4 * hdim):
            rows = jnp.dot(pick, buf[part, :, base : base + 4 * hdim], preferred_element_type=F32)
            if part == 3:
                rows = rows * gate
            rows = rows.astype(BF16)
            for i in range(4):
                out[base // hdim + i, part] = rows[:, i * hdim : (i + 1) * hdim]
        send = pltpu.make_async_copy(out.at[:, part], out_hbm.at[:, part], out_sems.at[part])
        send.start()
        sends.append(send)
    for send in sends:
        send.wait()


def compact_kernel(before_ref, in_ref, out_ref, buf):
    shards, slots, _ = in_ref.shape
    total = out_ref.shape[0]
    for c in range(shards):
        buf[pl.ds(before_ref[c], slots), :] = in_ref[c].astype(F32)
    out_ref[...] = buf[:total, :].astype(BF16)


def fold(x, op):
    return op(x.reshape(x.shape[0] // 8, 8, x.shape[1]), axis=0)


def strips(lo):
    return [slice(a, a + STRIP) for a in range(0, lo + BLK, STRIP)]


def sort_arrays(here_ref, arr, refs):
    role = lax.rem(here_ref[0], PARTS)
    for i, ref in enumerate(refs):
        arr[role ^ i] = ref[...]
    return role, lax.div(here_ref[0], PARTS), [arr.at[i] for i in range(PARTS)]


def raw_scores(k_ref, q_ref, rbuf, lo):
    n = lo + BLK
    raw = lax.dot_general(k_ref[:n, :], q_ref[lo:n, :], NT, preferred_element_type=F32)
    tri = lax.broadcasted_iota(jnp.int32, (BLK, BLK), 0) <= lax.broadcasted_iota(
        jnp.int32, (BLK, BLK), 1
    )
    if lo:
        rbuf[:lo, lo:n] = raw[:lo, :]
    rbuf[lo:n, lo:n] = jnp.where(tri, raw[lo:, :], FAR)


def products(v_ref, g_ref, gbuf, lo):
    n = lo + BLK
    gbuf[:n, lo:n] = lax.dot_general(v_ref[:n, :], g_ref[lo:n, :], NT, preferred_element_type=F32)


def stats_kernel(
    here_ref, scale_ref, x0, x1, x2, x3, ds_ref, att_ref, lse_ref, delta_ref, arr, pbuf, rbuf, gbuf
):
    total, hdim = x0.shape
    inv = 1.0 / math.sqrt(hdim)
    _, head, (q_ref, k_ref, v_ref, g_ref) = sort_arrays(here_ref, arr, (x0, x1, x2, x3))
    coef2 = scale_ref[head] * (inv * math.log2(math.e))
    blocks = range(0, total, BLK)
    for lo in blocks:
        raw_scores(k_ref, q_ref, rbuf, lo)
    vt = v_ref[...].astype(F32).T.astype(BF16)
    lses = []
    for lo in blocks:
        cols = slice(lo, lo + BLK)
        top = jnp.full((8, BLK), -jnp.inf, F32)
        for rows in strips(lo):
            top = jnp.maximum(top, fold(rbuf[rows, cols], jnp.max))
        top = jnp.max(top, axis=0, keepdims=True) * coef2
        acc = jnp.zeros((8, BLK), F32)
        for rows in strips(lo):
            acc = acc + fold(jnp.exp2(rbuf[rows, cols] * coef2 - top), jnp.sum)
        lse = top + jnp.log2(jnp.sum(acc, axis=0, keepdims=True))
        for rows in strips(lo):
            pbuf[rows, cols] = jnp.exp2(rbuf[rows, cols] * coef2 - lse).astype(BF16)
        lse_ref[:, cols] = lse
        lses.append(lse)
        products(v_ref, g_ref, gbuf, lo)
    deltas = []
    for lo in blocks:
        n = lo + BLK
        att = jnp.dot(vt[:, :n], pbuf[:n, lo:n], preferred_element_type=F32).astype(BF16)
        att_ref[:, lo:n] = att
        git = g_ref[lo:n, :].astype(F32).T
        delta = jnp.sum(git * att.astype(F32), axis=0, keepdims=True)
        delta_ref[:, lo:n] = delta
        deltas.append(delta)
    dsc = jnp.zeros((8, BLK), F32)
    for lo, lse, delta in zip(blocks, lses, deltas):
        cols = slice(lo, lo + BLK)
        for rows in strips(lo):
            raw = rbuf[rows, cols]
            ds = jnp.exp2(raw * coef2 - lse) * (gbuf[rows, cols] - delta)
            dsc = dsc + fold(ds * raw, jnp.sum)
    mine = lax.broadcasted_iota(jnp.int32, ds_ref.shape, 2) == head
    dsum = jnp.sum(jnp.sum(dsc, axis=0, keepdims=True), axis=1, keepdims=True) * inv
    ds_ref[...] = jnp.where(mine, dsum.reshape(1, 1, 1), 0.0)


def grads_kernel(
    before_ref, here_ref, scale_ref, x0, x1, x2, x3, att_ref, lse_ref, delta_ref, out_ref, arr, res, wbuf, rbuf, gbuf
):
    shards, slots, hdim = out_ref.shape
    total = x0.shape[0]
    inv = 1.0 / math.sqrt(hdim)
    role, head, (q_ref, k_ref, v_ref, g_ref) = sort_arrays(here_ref, arr, (x0, x1, x2, x3))
    coef = scale_ref[head] * inv
    coef2 = coef * math.log2(math.e)
    blocks = range(0, total, BLK)

    @pl.when(role == 0)
    def _():
        res[:total, :] = att_ref[...].astype(F32).T

    @pl.when(role == 3)
    def _():
        for lo in blocks:
            raw_scores(k_ref, q_ref, rbuf, lo)
        for lo in blocks:
            cols = slice(lo, lo + BLK)
            lse = lse_ref[:, cols]
            for rows in strips(lo):
                wbuf[rows, cols] = jnp.exp2(rbuf[rows, cols] * coef2 - lse).astype(BF16)
        for lo in blocks:
            res[lo : lo + BLK, :] = jnp.dot(
                wbuf[lo : lo + BLK, lo:], g_ref[lo:, :], preferred_element_type=F32
            )

    @pl.when((role == 1) | (role == 2))
    def _():
        for lo in blocks:
            raw_scores(k_ref, q_ref, rbuf, lo)
            products(v_ref, g_ref, gbuf, lo)
        for lo in blocks:
            cols = slice(lo, lo + BLK)
            lse = lse_ref[:, cols]
            delta = delta_ref[:, cols]
            for rows in strips(lo):
                p = jnp.exp2(rbuf[rows, cols] * coef2 - lse)
                wbuf[rows, cols] = (p * (gbuf[rows, cols] - delta)).astype(BF16)

    @pl.when(role == 1)
    def _():
        kt = k_ref[...].astype(F32).T.astype(BF16)
        for lo in blocks:
            n = lo + BLK
            dq = jnp.dot(kt[:, :n], wbuf[:n, lo:n], preferred_element_type=F32)
            res[lo:n, :] = (coef * dq).T

    @pl.when(role == 2)
    def _():
        for lo in blocks:
            res[lo : lo + BLK, :] = coef * jnp.dot(
                wbuf[lo : lo + BLK, lo:], q_ref[lo:, :], preferred_element_type=F32
            )

    res[total:, :] = jnp.zeros((slots, hdim), F32)
    for c in range(shards):
        out_ref[c] = res[pl.ds(before_ref[c], slots), :].astype(BF16)


def place_kernel(
    here_ref, places_ref, logit_ref, g_ref, in_ref, bo_ref, dq_ref, dk_ref, dv_ref, dl_ref
):
    tok, width = g_ref.shape
    slots, hdim = in_ref.shape[1:]
    col = slot_column(places_ref[...], here_ref[0] * tok, tok)
    hit = lax.broadcasted_iota(jnp.int32, (tok, slots), 1).astype(F32) + 1.0 == col
    spread = hit.astype(BF16)
    gate_row = sigmoid(logit_ref[...])
    gate = to_col(gate_row, tok)
    acc = jnp.zeros((tok, 2 * hdim), F32)
    for head in range(0, width // hdim, 2):
        cols = slice(head * hdim, (head + 2) * hdim)

        def home(part):
            pair = [in_ref[(head + i) * PARTS + part] for i in range(2)]
            return jnp.dot(spread, jnp.concatenate(pair, axis=1), preferred_element_type=F32)

        att = home(0)
        bo_ref[:, cols] = (gate * att).astype(BF16)
        acc = acc + g_ref[:, cols].astype(F32) * att
        dq_ref[:, cols] = home(1).astype(BF16)
        dk_ref[:, cols] = home(2).astype(BF16)
        dv_ref[:, cols] = home(3).astype(BF16)
    dot = to_row(jnp.sum(acc, axis=1, keepdims=True), tok)
    dl_ref[...] = gate_row * (1.0 - gate_row) * dot


def body(queries, keys, values, router_logit, head_scale, routed, grad_out):
    nctx = lax.axis_size("ctx")
    here = lax.axis_index("ctx")
    tok, width = queries.shape[1:]
    heads = head_scale.shape[0]
    hdim = width // heads
    total = routed.shape[1]
    rows = total // nctx
    slots = rows + 3 * (rows // 2)
    here_vec = here.astype(jnp.int32)[None]
    starts = jnp.arange(nctx, dtype=jnp.int32) * tok
    before = jnp.sum((routed[0][None, :] < starts[:, None]).astype(jnp.int32), axis=1)
    params = pltpu.CompilerParams(vmem_limit_bytes=24 * 1024 * 1024)

    send = pl.pallas_call(
        pack_kernel,
        out_shape=jax.ShapeDtypeStruct((heads, PARTS, slots, hdim), BF16),
        in_specs=[SM] + [HB] * 6,
        out_specs=HB,
        scratch_shapes=[
            pltpu.VMEM((1, total), jnp.int32),
            pltpu.VMEM((1, tok), F32),
            pltpu.VMEM((PARTS, tok, width), BF16),
            pltpu.VMEM((heads, PARTS, slots, hdim), BF16),
            pltpu.SemaphoreType.DMA((PARTS + 2,)),
            pltpu.SemaphoreType.DMA((PARTS,)),
        ],
        compiler_params=pltpu.CompilerParams(vmem_limit_bytes=60 * 1024 * 1024),
        name="pack",
    )(here_vec, routed, router_logit, queries[0], keys[0], values[0], grad_out[0])
    send = send.reshape(nctx, slots, hdim)
    got = lax.all_to_all(send, "ctx", split_axis=0, concat_axis=0, tiled=True)
    own = pl.pallas_call(
        compact_kernel,
        out_shape=jax.ShapeDtypeStruct((total, hdim), BF16),
        in_specs=[SM, VM],
        out_specs=VM,
        scratch_shapes=[pltpu.VMEM((total + slots, hdim), F32)],
        compiler_params=params,
        name="compact",
    )(before, got)
    side = lax.ppermute(own, "ctx", [(i, i ^ 2) for i in range(nctx)])
    near = lax.ppermute(own, "ctx", [(i, i ^ 1) for i in range(nctx)])
    cross = lax.ppermute(side, "ctx", [(i, i ^ 1) for i in range(nctx)])
    arrays = (own, near, side, cross)
    table = [
        pltpu.VMEM((PARTS, total, hdim), BF16),
        pltpu.VMEM((total, total), BF16),
        pltpu.VMEM((total, total), F32),
        pltpu.VMEM((total, total), F32),
    ]
    dsc, att, lse, delta = pl.pallas_call(
        stats_kernel,
        out_shape=(
            jax.ShapeDtypeStruct((heads, 1, 128), F32),
            jax.ShapeDtypeStruct((hdim, total), BF16),
            jax.ShapeDtypeStruct((1, total), F32),
            jax.ShapeDtypeStruct((1, total), F32),
        ),
        in_specs=[SM] * 2 + [VM] * 4,
        out_specs=(VM,) * 4,
        scratch_shapes=table,
        compiler_params=params,
        name="stats",
    )(here_vec, head_scale, *arrays)
    back = pl.pallas_call(
        grads_kernel,
        out_shape=jax.ShapeDtypeStruct((nctx, slots, hdim), BF16),
        in_specs=[SM] * 3 + [VM] * 7,
        out_specs=VM,
        scratch_shapes=[table[0], pltpu.VMEM((total + slots, hdim), F32)] + table[1:],
        compiler_params=params,
        name="grads",
    )(before, here_vec, head_scale, *arrays, att, lse, delta)
    groups = [[PARTS * i + j for i in range(heads)] for j in range(nctx // heads)]
    dsc = lax.all_to_all(
        dsc,
        "ctx",
        split_axis=0,
        concat_axis=0,
        axis_index_groups=groups,
        tiled=True,
    )
    back, dsc = lax.optimization_barrier((back, dsc))
    home = lax.all_to_all(back, "ctx", split_axis=0, concat_axis=0, tiled=True)
    dsc = lax.psum(jnp.sum(dsc, axis=0)[:, :heads], "dp")
    home, dsc = lax.optimization_barrier((home, dsc))
    outs = pl.pallas_call(
        place_kernel,
        out_shape=tuple([jax.ShapeDtypeStruct((tok, width), BF16)] * 4)
        + (jax.ShapeDtypeStruct((1, tok), F32),),
        in_specs=[SM] + [VM] * 4,
        out_specs=(VM,) * 5,
        compiler_params=params,
        name="place",
    )(here_vec, routed, router_logit, grad_out[0], home)
    block_out, d_q, d_k, d_v, d_logit = outs
    return block_out[None], d_q[None], d_k[None], d_v[None], d_logit, dsc[0]


def solution(mesh):
    in_specs = (
        P("dp", "ctx", None),
        P("dp", "ctx", None),
        P("dp", "ctx", None),
        P("dp", "ctx"),
        P(),
        P("dp", None),
        P("dp", "ctx", None),
    )
    out_specs = (
        P("dp", "ctx", None),
        P("dp", "ctx", None),
        P("dp", "ctx", None),
        P("dp", "ctx", None),
        P("dp", "ctx"),
        P(),
    )
    return jax.shard_map(body, mesh=mesh, in_specs=in_specs, out_specs=out_specs, check_vma=False)
```

```python
import functools
import math

import jax
import jax.numpy as jnp
from jax import lax
from jax.experimental import pallas as pl
from jax.experimental.pallas import tpu as pltpu
from jax.sharding import PartitionSpec as P

F32 = jnp.float32
BF16 = jnp.bfloat16
VM = pl.BlockSpec(memory_space=pltpu.VMEM)
SM = pl.BlockSpec(memory_space=pltpu.SMEM)
HB = pl.BlockSpec(memory_space=pltpu.HBM)
NT = (((1,), (1,)), ((), ()))
PARTS = 4
FAR = -3e38
BLK = 256
STRIP = 32


def eye(n):
    return lax.broadcasted_iota(jnp.int32, (n, n), 0) == lax.broadcasted_iota(jnp.int32, (n, n), 1)


def to_row(col, n):
    return jnp.sum(jnp.where(eye(n), col, 0.0), axis=0, keepdims=True)


def to_col(row, n):
    return jnp.sum(jnp.where(eye(n), row, 0.0), axis=1, keepdims=True)


def slot_column(places, first, tok):
    total = places.shape[1]
    before = jnp.sum((places < first).astype(F32), axis=1, keepdims=True)
    rank = lax.broadcasted_iota(jnp.int32, (1, total), 1).astype(F32) + 1.0 - before
    here = places - first == lax.broadcasted_iota(jnp.int32, (tok, total), 0)
    return jnp.sum(jnp.where(here, rank, 0.0), axis=1, keepdims=True)


def sigmoid(x):
    return 1.0 / (1.0 + jnp.exp(-x))


def pack_kernel(
    here_ref, places_hbm, logit_hbm, q_hbm, k_hbm, v_hbm, g_hbm, out_hbm, places, logit, buf, out, sems, out_sems
):
    tok, width = q_hbm.shape
    heads, _, slots, hdim = out.shape
    small = [
        pltpu.make_async_copy(src, dst, sems.at[PARTS + i])
        for i, (src, dst) in enumerate(((places_hbm, places), (logit_hbm, logit)))
    ]
    copies = [
        pltpu.make_async_copy(ref, buf.at[part], sems.at[part])
        for part, ref in enumerate((q_hbm, k_hbm, v_hbm, g_hbm))
    ]
    for copy in small + copies:
        copy.start()
    for copy in small:
        copy.wait()
    row = to_row(slot_column(places[...], here_ref[0] * tok, tok), tok)
    hit = lax.broadcasted_iota(jnp.int32, (slots, tok), 0).astype(F32) + 1.0 == row
    pick = hit.astype(BF16)
    gate = jnp.sum(jnp.where(hit, sigmoid(logit[...]), 0.0), axis=1, keepdims=True)
    sends = []
    for part, copy in enumerate(copies):
        copy.wait()
        for base in range(0, width, 4 * hdim):
            rows = jnp.dot(pick, buf[part, :, base : base + 4 * hdim], preferred_element_type=F32)
            if part == 3:
                rows = rows * gate
            rows = rows.astype(BF16)
            for i in range(4):
                out[base // hdim + i, part] = rows[:, i * hdim : (i + 1) * hdim]
        send = pltpu.make_async_copy(out.at[:, part], out_hbm.at[:, part], out_sems.at[part])
        send.start()
        sends.append(send)
    for send in sends:
        send.wait()


def compact_kernel(before_ref, in_ref, out_ref, buf):
    shards, slots, _ = in_ref.shape
    total = out_ref.shape[0]
    for c in range(shards):
        buf[pl.ds(before_ref[c], slots), :] = in_ref[c].astype(F32)
    out_ref[...] = buf[:total, :].astype(BF16)


def fold(x, op):
    return op(x.reshape(x.shape[0] // 8, 8, x.shape[1]), axis=0)


def strips(lo):
    return [slice(a, a + STRIP) for a in range(0, lo + BLK, STRIP)]


def raw_scores(k_ref, q_ref, rbuf, lo):
    n = lo + BLK
    raw = lax.dot_general(k_ref[:n, :], q_ref[lo:n, :], NT, preferred_element_type=F32)
    tri = lax.broadcasted_iota(jnp.int32, (BLK, BLK), 0) <= lax.broadcasted_iota(
        jnp.int32, (BLK, BLK), 1
    )
    if lo:
        rbuf[:lo, lo:n] = raw[:lo, :]
    rbuf[lo:n, lo:n] = jnp.where(tri, raw[lo:, :], FAR)


def products(v_ref, g_ref, gbuf, lo):
    n = lo + BLK
    gbuf[:n, lo:n] = lax.dot_general(v_ref[:n, :], g_ref[lo:n, :], NT, preferred_element_type=F32)


def forward(refs, rbuf, pbuf, gbuf, coef2, att_ref, lse_ref, delta_ref):
    q_ref, k_ref, v_ref, g_ref = refs
    blocks = range(0, q_ref.shape[0], BLK)
    for lo in blocks:
        raw_scores(k_ref, q_ref, rbuf, lo)
    vt = v_ref[...].astype(F32).T.astype(BF16)
    lses = []
    for lo in blocks:
        cols = slice(lo, lo + BLK)
        top = jnp.full((8, BLK), -jnp.inf, F32)
        for rows in strips(lo):
            top = jnp.maximum(top, fold(rbuf[rows, cols], jnp.max))
        top = jnp.max(top, axis=0, keepdims=True) * coef2
        acc = jnp.zeros((8, BLK), F32)
        for rows in strips(lo):
            acc = acc + fold(jnp.exp2(rbuf[rows, cols] * coef2 - top), jnp.sum)
        lse = top + jnp.log2(jnp.sum(acc, axis=0, keepdims=True))
        for rows in strips(lo):
            pbuf[rows, cols] = jnp.exp2(rbuf[rows, cols] * coef2 - lse).astype(BF16)
        lse_ref[:, cols] = lse
        lses.append(lse)
        products(v_ref, g_ref, gbuf, lo)
    deltas = []
    for lo in blocks:
        n = lo + BLK
        att = jnp.dot(vt[:, :n], pbuf[:n, lo:n], preferred_element_type=F32).astype(BF16)
        att_ref[:, lo:n] = att
        git = g_ref[lo:n, :].astype(F32).T
        delta = jnp.sum(git * att.astype(F32), axis=0, keepdims=True)
        delta_ref[:, lo:n] = delta
        deltas.append(delta)
    return lses, deltas


def stats_kernel(
    here_ref, scale_ref, x0, x1, x2, x3, ds_ref, att_ref, lse_ref, delta_ref, rest_ref, arr, pbuf, rbuf, gbuf
):
    total, hdim = x0.shape
    inv = 1.0 / math.sqrt(hdim)
    ds_ref[...] = jnp.zeros_like(ds_ref)

    @pl.when(lax.rem(here_ref[0], 2) == 0)
    def _():
        role = lax.rem(here_ref[0], PARTS)
        head = lax.div(here_ref[0], PARTS)
        for i, ref in enumerate((x0, x1, x2, x3)):
            arr[role ^ i] = ref[...]
        rest_ref[0] = x2[...]
        rest_ref[1] = x3[...]
        coef2 = scale_ref[head] * (inv * math.log2(math.e))
        refs = [arr.at[i] for i in range(PARTS)]
        lses, deltas = forward(refs, rbuf, pbuf, gbuf, coef2, att_ref, lse_ref, delta_ref)
        dsc = jnp.zeros((8, BLK), F32)
        for lo, lse, delta in zip(range(0, total, BLK), lses, deltas):
            cols = slice(lo, lo + BLK)
            for rows in strips(lo):
                raw = rbuf[rows, cols]
                ds = jnp.exp2(raw * coef2 - lse) * (gbuf[rows, cols] - delta)
                dsc = dsc + fold(ds * raw, jnp.sum)
        mine = lax.broadcasted_iota(jnp.int32, ds_ref.shape, 2) == head
        dsum = jnp.sum(jnp.sum(dsc, axis=0, keepdims=True), axis=1, keepdims=True) * inv
        ds_ref[...] = jnp.where(mine, dsum.reshape(1, 1, 1), 0.0)


def grads_kernel(
    before_ref, here_ref, scale_ref, x0, x1, x2, x3, got, att_ref, lse_ref, delta_ref, out_ref,
    arr, res, pbuf, rbuf, gbuf, wbuf, att_own, lse_own, delta_own,
):
    shards, slots, hdim = out_ref.shape
    total = x0.shape[0]
    inv = 1.0 / math.sqrt(hdim)
    role = lax.rem(here_ref[0], PARTS)
    coef = scale_ref[lax.div(here_ref[0], PARTS)] * inv
    coef2 = coef * math.log2(math.e)
    blocks = range(0, total, BLK)
    refs = [arr.at[i] for i in range(PARTS)]
    q_ref, k_ref, v_ref, g_ref = refs
    arr[role] = x0[...]
    arr[role ^ 1] = x1[...]

    def fill(lse_of, delta_of):
        for lo in blocks:
            cols = slice(lo, lo + BLK)
            lse = lse_of[:, cols]
            delta = delta_of[:, cols]
            for rows in strips(lo):
                p = jnp.exp2(rbuf[rows, cols] * coef2 - lse)
                wbuf[rows, cols] = (p * (gbuf[rows, cols] - delta)).astype(BF16)

    @pl.when(role == 0)
    def _():
        res[:total, :] = att_ref[...].astype(F32).T

    @pl.when(role == 2)
    def _():
        arr[role ^ 2] = x2[...]
        arr[role ^ 3] = x3[...]
        for lo in blocks:
            raw_scores(k_ref, q_ref, rbuf, lo)
            products(v_ref, g_ref, gbuf, lo)
        fill(lse_ref, delta_ref)
        for lo in blocks:
            res[lo : lo + BLK, :] = coef * jnp.dot(
                wbuf[lo : lo + BLK, lo:], q_ref[lo:, :], preferred_element_type=F32
            )

    @pl.when(lax.rem(role, 2) == 1)
    def _():
        arr[role ^ 2] = got[1]
        arr[role ^ 3] = got[0]
        forward(refs, rbuf, pbuf, gbuf, coef2, att_own, lse_own, delta_own)

    @pl.when(role == 1)
    def _():
        fill(lse_own, delta_own)
        kt = k_ref[...].astype(F32).T.astype(BF16)
        for lo in blocks:
            n = lo + BLK
            dq = jnp.dot(kt[:, :n], wbuf[:n, lo:n], preferred_element_type=F32)
            res[lo:n, :] = (coef * dq).T

    @pl.when(role == 3)
    def _():
        for lo in blocks:
            res[lo : lo + BLK, :] = jnp.dot(
                pbuf[lo : lo + BLK, lo:], g_ref[lo:, :], preferred_element_type=F32
            )

    res[total:, :] = jnp.zeros((slots, hdim), F32)
    for c in range(shards):
        out_ref[c] = res[pl.ds(before_ref[c], slots), :].astype(BF16)


def place_kernel(
    here_ref, places_ref, logit_ref, g_ref, in_ref, bo_ref, dq_ref, dk_ref, dv_ref, dl_ref
):
    tok, width = g_ref.shape
    slots, hdim = in_ref.shape[1:]
    col = slot_column(places_ref[...], here_ref[0] * tok, tok)
    hit = lax.broadcasted_iota(jnp.int32, (tok, slots), 1).astype(F32) + 1.0 == col
    spread = hit.astype(BF16)
    gate_row = sigmoid(logit_ref[...])
    gate = to_col(gate_row, tok)
    acc = jnp.zeros((tok, 2 * hdim), F32)
    for head in range(0, width // hdim, 2):
        cols = slice(head * hdim, (head + 2) * hdim)

        def home(part):
            pair = [in_ref[(head + i) * PARTS + part] for i in range(2)]
            return jnp.dot(spread, jnp.concatenate(pair, axis=1), preferred_element_type=F32)

        att = home(0)
        bo_ref[:, cols] = (gate * att).astype(BF16)
        acc = acc + g_ref[:, cols].astype(F32) * att
        dq_ref[:, cols] = home(1).astype(BF16)
        dk_ref[:, cols] = home(2).astype(BF16)
        dv_ref[:, cols] = home(3).astype(BF16)
    dot = to_row(jnp.sum(acc, axis=1, keepdims=True), tok)
    dl_ref[...] = gate_row * (1.0 - gate_row) * dot


def body(queries, keys, values, router_logit, head_scale, routed, grad_out):
    nctx = lax.axis_size("ctx")
    here = lax.axis_index("ctx")
    tok, width = queries.shape[1:]
    heads = head_scale.shape[0]
    hdim = width // heads
    total = routed.shape[1]
    rows = total // nctx
    slots = rows + 3 * (rows // 2)
    here_vec = here.astype(jnp.int32)[None]
    starts = jnp.arange(nctx, dtype=jnp.int32) * tok
    before = jnp.sum((routed[0][None, :] < starts[:, None]).astype(jnp.int32), axis=1)
    params = pltpu.CompilerParams(vmem_limit_bytes=24 * 1024 * 1024)

    send = pl.pallas_call(
        pack_kernel,
        out_shape=jax.ShapeDtypeStruct((heads, PARTS, slots, hdim), BF16),
        in_specs=[SM] + [HB] * 6,
        out_specs=HB,
        scratch_shapes=[
            pltpu.VMEM((1, total), jnp.int32),
            pltpu.VMEM((1, tok), F32),
            pltpu.VMEM((PARTS, tok, width), BF16),
            pltpu.VMEM((heads, PARTS, slots, hdim), BF16),
            pltpu.SemaphoreType.DMA((PARTS + 2,)),
            pltpu.SemaphoreType.DMA((PARTS,)),
        ],
        compiler_params=pltpu.CompilerParams(vmem_limit_bytes=60 * 1024 * 1024),
        name="pack",
    )(here_vec, routed, router_logit, queries[0], keys[0], values[0], grad_out[0])
    send = send.reshape(nctx, slots, hdim)
    got = lax.all_to_all(send, "ctx", split_axis=0, concat_axis=0, tiled=True)
    own = pl.pallas_call(
        compact_kernel,
        out_shape=jax.ShapeDtypeStruct((total, hdim), BF16),
        in_specs=[SM, VM],
        out_specs=VM,
        scratch_shapes=[pltpu.VMEM((total + slots, hdim), F32)],
        compiler_params=params,
        name="compact",
    )(before, got)
    odd = list(range(1, nctx, 2))
    even = list(range(0, nctx, 2))
    side = lax.ppermute(own, "ctx", [(i, i ^ 2) for i in even])
    cross = lax.ppermute(own, "ctx", [(i, i ^ 3) for i in odd])
    near = lax.ppermute(own, "ctx", [(i, i ^ 1) for i in range(nctx)])
    arrays = (own, near, side, cross)
    table = [
        pltpu.VMEM((PARTS, total, hdim), BF16),
        pltpu.VMEM((total, total), BF16),
        pltpu.VMEM((total, total), F32),
        pltpu.VMEM((total, total), F32),
    ]
    dsc, att, lse, delta, rest = pl.pallas_call(
        stats_kernel,
        out_shape=(
            jax.ShapeDtypeStruct((nctx // 2, 1, 128), F32),
            jax.ShapeDtypeStruct((hdim, total), BF16),
            jax.ShapeDtypeStruct((1, total), F32),
            jax.ShapeDtypeStruct((1, total), F32),
            jax.ShapeDtypeStruct((2, total, hdim), BF16),
        ),
        in_specs=[SM] * 2 + [VM] * 4,
        out_specs=(VM,) * 5,
        scratch_shapes=table,
        compiler_params=params,
        name="stats",
    )(here_vec, head_scale, *arrays)
    got_rest = lax.ppermute(rest, "ctx", [(i, i ^ 1) for i in even])
    back = pl.pallas_call(
        grads_kernel,
        out_shape=jax.ShapeDtypeStruct((nctx, slots, hdim), BF16),
        in_specs=[SM] * 3 + [VM] * 8,
        out_specs=VM,
        scratch_shapes=[table[0], pltpu.VMEM((total + slots, hdim), F32)]
        + table[1:]
        + [
            table[1],
            pltpu.VMEM((hdim, total), BF16),
            pltpu.VMEM((1, total), F32),
            pltpu.VMEM((1, total), F32),
        ],
        compiler_params=params,
        name="grads",
    )(before, here_vec, head_scale, *arrays, got_rest, att, lse, delta)
    groups = [[i for i in range(nctx) if i // 2 % 2 == j] for j in range(2)]
    dsc = lax.all_to_all(
        dsc,
        "ctx",
        split_axis=0,
        concat_axis=0,
        axis_index_groups=groups,
        tiled=True,
    )
    back, dsc = lax.optimization_barrier((back, dsc))
    home = lax.all_to_all(back, "ctx", split_axis=0, concat_axis=0, tiled=True)
    dsc = lax.psum(jnp.sum(dsc, axis=0)[:, :heads], "dp")
    home, dsc = lax.optimization_barrier((home, dsc))
    outs = pl.pallas_call(
        place_kernel,
        out_shape=tuple([jax.ShapeDtypeStruct((tok, width), BF16)] * 4)
        + (jax.ShapeDtypeStruct((1, tok), F32),),
        in_specs=[SM] + [VM] * 4,
        out_specs=(VM,) * 5,
        compiler_params=params,
        name="place",
    )(here_vec, routed, router_logit, grad_out[0], home)
    block_out, d_q, d_k, d_v, d_logit = outs
    return block_out[None], d_q[None], d_k[None], d_v[None], d_logit, dsc[0]


def solution(mesh):
    in_specs = (
        P("dp", "ctx", None),
        P("dp", "ctx", None),
        P("dp", "ctx", None),
        P("dp", "ctx"),
        P(),
        P("dp", None),
        P("dp", "ctx", None),
    )
    out_specs = (
        P("dp", "ctx", None),
        P("dp", "ctx", None),
        P("dp", "ctx", None),
        P("dp", "ctx", None),
        P("dp", "ctx"),
        P(),
    )
    return jax.shard_map(body, mesh=mesh, in_specs=in_specs, out_specs=out_specs, check_vma=False)
```

```python
import functools
import math

import jax
import jax.numpy as jnp
from jax import lax
from jax.experimental import pallas as pl
from jax.experimental.pallas import tpu as pltpu
from jax.sharding import PartitionSpec as P

F32 = jnp.float32
BF16 = jnp.bfloat16
VM = pl.BlockSpec(memory_space=pltpu.VMEM)
SM = pl.BlockSpec(memory_space=pltpu.SMEM)
HB = pl.BlockSpec(memory_space=pltpu.HBM)
NT = (((1,), (1,)), ((), ()))
PARTS = 4
FAR = -3e38
BLK = 256
STRIP = 32


def eye(n):
    return lax.broadcasted_iota(jnp.int32, (n, n), 0) == lax.broadcasted_iota(jnp.int32, (n, n), 1)


def to_row(col, n):
    return jnp.sum(jnp.where(eye(n), col, 0.0), axis=0, keepdims=True)


def to_col(row, n):
    return jnp.sum(jnp.where(eye(n), row, 0.0), axis=1, keepdims=True)


def slot_column(places, first, tok):
    total = places.shape[1]
    before = jnp.sum((places < first).astype(F32), axis=1, keepdims=True)
    rank = lax.broadcasted_iota(jnp.int32, (1, total), 1).astype(F32) + 1.0 - before
    here = places - first == lax.broadcasted_iota(jnp.int32, (tok, total), 0)
    return jnp.sum(jnp.where(here, rank, 0.0), axis=1, keepdims=True)


def sigmoid(x):
    return 1.0 / (1.0 + jnp.exp(-x))


def pack_kernel(
    here_ref, places_hbm, logit_hbm, q_hbm, k_hbm, v_hbm, g_hbm, out_ref, places, logit, buf, sems
):
    tok, width = q_hbm.shape
    slots, hdim = out_ref.shape[1:]
    small = [
        pltpu.make_async_copy(src, dst, sems.at[PARTS + i])
        for i, (src, dst) in enumerate(((places_hbm, places), (logit_hbm, logit)))
    ]
    copies = [
        pltpu.make_async_copy(ref, buf.at[part], sems.at[part])
        for part, ref in enumerate((q_hbm, k_hbm, v_hbm, g_hbm))
    ]
    for copy in small + copies:
        copy.start()
    for copy in small:
        copy.wait()
    row = to_row(slot_column(places[...], here_ref[0] * tok, tok), tok)
    hit = lax.broadcasted_iota(jnp.int32, (slots, tok), 0).astype(F32) + 1.0 == row
    pick = hit.astype(BF16)
    gate = jnp.sum(jnp.where(hit, sigmoid(logit[...]), 0.0), axis=1, keepdims=True)
    for part, copy in enumerate(copies):
        copy.wait()
        for base in range(0, width, 4 * hdim):
            rows = jnp.dot(pick, buf[part, :, base : base + 4 * hdim], preferred_element_type=F32)
            if part == 3:
                rows = rows * gate
            rows = rows.astype(BF16)
            for i in range(4):
                head = base // hdim + i
                out_ref[head * PARTS + part] = rows[:, i * hdim : (i + 1) * hdim]


def compact_kernel(before_ref, in_ref, out_ref, buf):
    shards, slots, _ = in_ref.shape
    total = out_ref.shape[0]
    for c in range(shards):
        buf[pl.ds(before_ref[c], slots), :] = in_ref[c].astype(F32)
    out_ref[...] = buf[:total, :].astype(BF16)


def fold(x, op):
    return op(x.reshape(x.shape[0] // 8, 8, x.shape[1]), axis=0)


def strips(lo):
    return [slice(a, a + STRIP) for a in range(0, lo + BLK, STRIP)]


def raw_scores(k_ref, q_ref, rbuf, lo):
    n = lo + BLK
    raw = lax.dot_general(k_ref[:n, :], q_ref[lo:n, :], NT, preferred_element_type=F32)
    tri = lax.broadcasted_iota(jnp.int32, (BLK, BLK), 0) <= lax.broadcasted_iota(
        jnp.int32, (BLK, BLK), 1
    )
    if lo:
        rbuf[:lo, lo:n] = raw[:lo, :]
    rbuf[lo:n, lo:n] = jnp.where(tri, raw[lo:, :], FAR)


def products(v_ref, g_ref, gbuf, lo):
    n = lo + BLK
    gbuf[:n, lo:n] = lax.dot_general(v_ref[:n, :], g_ref[lo:n, :], NT, preferred_element_type=F32)


def forward(refs, rbuf, pbuf, gbuf, coef2, att_ref, lse_ref, delta_ref):
    q_ref, k_ref, v_ref, g_ref = refs
    blocks = range(0, q_ref.shape[0], BLK)
    for lo in blocks:
        raw_scores(k_ref, q_ref, rbuf, lo)
    vt = v_ref[...].astype(F32).T.astype(BF16)
    lses = []
    for lo in blocks:
        cols = slice(lo, lo + BLK)
        top = jnp.full((8, BLK), -jnp.inf, F32)
        for rows in strips(lo):
            top = jnp.maximum(top, fold(rbuf[rows, cols], jnp.max))
        top = jnp.max(top, axis=0, keepdims=True) * coef2
        acc = jnp.zeros((8, BLK), F32)
        for rows in strips(lo):
            acc = acc + fold(jnp.exp2(rbuf[rows, cols] * coef2 - top), jnp.sum)
        lse = top + jnp.log2(jnp.sum(acc, axis=0, keepdims=True))
        for rows in strips(lo):
            pbuf[rows, cols] = jnp.exp2(rbuf[rows, cols] * coef2 - lse).astype(BF16)
        lse_ref[:, cols] = lse
        lses.append(lse)
        products(v_ref, g_ref, gbuf, lo)
    deltas = []
    for lo in blocks:
        n = lo + BLK
        att = jnp.dot(vt[:, :n], pbuf[:n, lo:n], preferred_element_type=F32).astype(BF16)
        att_ref[:, lo:n] = att
        git = g_ref[lo:n, :].astype(F32).T
        delta = jnp.sum(git * att.astype(F32), axis=0, keepdims=True)
        delta_ref[:, lo:n] = delta
        deltas.append(delta)
    return lses, deltas


def stats_kernel(
    here_ref, scale_ref, x0, x1, x2, x3, ds_ref, att_ref, lse_ref, delta_ref, rest_ref, arr, pbuf, rbuf, gbuf
):
    total, hdim = x0.shape
    inv = 1.0 / math.sqrt(hdim)
    ds_ref[...] = jnp.zeros_like(ds_ref)

    @pl.when(lax.rem(here_ref[0], 2) == 0)
    def _():
        role = lax.rem(here_ref[0], PARTS)
        head = lax.div(here_ref[0], PARTS)
        for i, ref in enumerate((x0, x1, x2, x3)):
            arr[role ^ i] = ref[...]
        rest_ref[0] = x2[...]
        rest_ref[1] = x3[...]
        coef2 = scale_ref[head] * (inv * math.log2(math.e))
        refs = [arr.at[i] for i in range(PARTS)]
        lses, deltas = forward(refs, rbuf, pbuf, gbuf, coef2, att_ref, lse_ref, delta_ref)
        dsc = jnp.zeros((8, BLK), F32)
        for lo, lse, delta in zip(range(0, total, BLK), lses, deltas):
            cols = slice(lo, lo + BLK)
            for rows in strips(lo):
                raw = rbuf[rows, cols]
                ds = jnp.exp2(raw * coef2 - lse) * (gbuf[rows, cols] - delta)
                dsc = dsc + fold(ds * raw, jnp.sum)
        mine = lax.broadcasted_iota(jnp.int32, ds_ref.shape, 2) == head
        dsum = jnp.sum(jnp.sum(dsc, axis=0, keepdims=True), axis=1, keepdims=True) * inv
        ds_ref[...] = jnp.where(mine, dsum.reshape(1, 1, 1), 0.0)


def grads_kernel(
    before_ref, here_ref, scale_ref, x0, x1, x2, x3, got, att_ref, lse_ref, delta_ref, out_ref,
    arr, res, pbuf, rbuf, gbuf, wbuf, att_own, lse_own, delta_own,
):
    shards, slots, hdim = out_ref.shape
    total = x0.shape[0]
    inv = 1.0 / math.sqrt(hdim)
    role = lax.rem(here_ref[0], PARTS)
    coef = scale_ref[lax.div(here_ref[0], PARTS)] * inv
    coef2 = coef * math.log2(math.e)
    blocks = range(0, total, BLK)
    refs = [arr.at[i] for i in range(PARTS)]
    q_ref, k_ref, v_ref, g_ref = refs
    arr[role] = x0[...]
    arr[role ^ 1] = x1[...]

    def fill(lse_of, delta_of):
        for lo in blocks:
            cols = slice(lo, lo + BLK)
            lse = lse_of[:, cols]
            delta = delta_of[:, cols]
            for rows in strips(lo):
                p = jnp.exp2(rbuf[rows, cols] * coef2 - lse)
                wbuf[rows, cols] = (p * (gbuf[rows, cols] - delta)).astype(BF16)

    @pl.when(role == 0)
    def _():
        res[:total, :] = att_ref[...].astype(F32).T

    @pl.when(role == 2)
    def _():
        arr[role ^ 2] = x2[...]
        arr[role ^ 3] = x3[...]
        for lo in blocks:
            raw_scores(k_ref, q_ref, rbuf, lo)
            products(v_ref, g_ref, gbuf, lo)
        fill(lse_ref, delta_ref)
        for lo in blocks:
            res[lo : lo + BLK, :] = coef * jnp.dot(
                wbuf[lo : lo + BLK, lo:], q_ref[lo:, :], preferred_element_type=F32
            )

    @pl.when(lax.rem(role, 2) == 1)
    def _():
        arr[role ^ 2] = got[1]
        arr[role ^ 3] = got[0]
        forward(refs, rbuf, pbuf, gbuf, coef2, att_own, lse_own, delta_own)

    @pl.when(role == 1)
    def _():
        fill(lse_own, delta_own)
        kt = k_ref[...].astype(F32).T.astype(BF16)
        for lo in blocks:
            n = lo + BLK
            dq = jnp.dot(kt[:, :n], wbuf[:n, lo:n], preferred_element_type=F32)
            res[lo:n, :] = (coef * dq).T

    @pl.when(role == 3)
    def _():
        for lo in blocks:
            res[lo : lo + BLK, :] = jnp.dot(
                pbuf[lo : lo + BLK, lo:], g_ref[lo:, :], preferred_element_type=F32
            )

    res[total:, :] = jnp.zeros((slots, hdim), F32)
    for c in range(shards):
        out_ref[c] = res[pl.ds(before_ref[c], slots), :].astype(BF16)


def place_kernel(
    here_ref, places_ref, logit_ref, g_ref, in_ref, bo_ref, dq_ref, dk_ref, dv_ref, dl_ref
):
    tok, width = g_ref.shape
    slots, hdim = in_ref.shape[1:]
    col = slot_column(places_ref[...], here_ref[0] * tok, tok)
    hit = lax.broadcasted_iota(jnp.int32, (tok, slots), 1).astype(F32) + 1.0 == col
    spread = hit.astype(BF16)
    gate_row = sigmoid(logit_ref[...])
    gate = to_col(gate_row, tok)
    acc = jnp.zeros((tok, 2 * hdim), F32)
    for head in range(0, width // hdim, 2):
        cols = slice(head * hdim, (head + 2) * hdim)

        def home(part):
            pair = [in_ref[(head + i) * PARTS + part] for i in range(2)]
            return jnp.dot(spread, jnp.concatenate(pair, axis=1), preferred_element_type=F32)

        att = home(0)
        bo_ref[:, cols] = (gate * att).astype(BF16)
        acc = acc + g_ref[:, cols].astype(F32) * att
        dq_ref[:, cols] = home(1).astype(BF16)
        dk_ref[:, cols] = home(2).astype(BF16)
        dv_ref[:, cols] = home(3).astype(BF16)
    dot = to_row(jnp.sum(acc, axis=1, keepdims=True), tok)
    dl_ref[...] = gate_row * (1.0 - gate_row) * dot


def body(queries, keys, values, router_logit, head_scale, routed, grad_out):
    nctx = lax.axis_size("ctx")
    here = lax.axis_index("ctx")
    tok, width = queries.shape[1:]
    heads = head_scale.shape[0]
    hdim = width // heads
    total = routed.shape[1]
    rows = total // nctx
    slots = rows + 3 * (rows // 2)
    here_vec = here.astype(jnp.int32)[None]
    starts = jnp.arange(nctx, dtype=jnp.int32) * tok
    before = jnp.sum((routed[0][None, :] < starts[:, None]).astype(jnp.int32), axis=1)
    params = pltpu.CompilerParams(vmem_limit_bytes=24 * 1024 * 1024)

    send = pl.pallas_call(
        pack_kernel,
        out_shape=jax.ShapeDtypeStruct((nctx, slots, hdim), BF16),
        in_specs=[SM] + [HB] * 6,
        out_specs=VM,
        scratch_shapes=[
            pltpu.VMEM((1, total), jnp.int32),
            pltpu.VMEM((1, tok), F32),
            pltpu.VMEM((PARTS, tok, width), BF16),
            pltpu.SemaphoreType.DMA((PARTS + 2,)),
        ],
        compiler_params=pltpu.CompilerParams(vmem_limit_bytes=60 * 1024 * 1024),
        name="pack",
    )(here_vec, routed, router_logit, queries[0], keys[0], values[0], grad_out[0])
    got = lax.all_to_all(send, "ctx", split_axis=0, concat_axis=0, tiled=True)
    own = pl.pallas_call(
        compact_kernel,
        out_shape=jax.ShapeDtypeStruct((total, hdim), BF16),
        in_specs=[SM, VM],
        out_specs=VM,
        scratch_shapes=[pltpu.VMEM((total + slots, hdim), F32)],
        compiler_params=params,
        name="compact",
    )(before, got)
    odd = list(range(1, nctx, 2))
    even = list(range(0, nctx, 2))
    side = lax.ppermute(own, "ctx", [(i, i ^ 2) for i in even])
    cross = lax.ppermute(own, "ctx", [(i, i ^ 3) for i in odd])
    near = lax.ppermute(own, "ctx", [(i, i ^ 1) for i in range(nctx)])
    arrays = (own, near, side, cross)
    table = [
        pltpu.VMEM((PARTS, total, hdim), BF16),
        pltpu.VMEM((total, total), BF16),
        pltpu.VMEM((total, total), F32),
        pltpu.VMEM((total, total), F32),
    ]
    dsc, att, lse, delta, rest = pl.pallas_call(
        stats_kernel,
        out_shape=(
            jax.ShapeDtypeStruct((nctx // 2, 1, 128), F32),
            jax.ShapeDtypeStruct((hdim, total), BF16),
            jax.ShapeDtypeStruct((1, total), F32),
            jax.ShapeDtypeStruct((1, total), F32),
            jax.ShapeDtypeStruct((2, total, hdim), BF16),
        ),
        in_specs=[SM] * 2 + [VM] * 4,
        out_specs=(VM,) * 5,
        scratch_shapes=table,
        compiler_params=params,
        name="stats",
    )(here_vec, head_scale, *arrays)
    got_rest = lax.ppermute(rest, "ctx", [(i, i ^ 1) for i in even])
    back = pl.pallas_call(
        grads_kernel,
        out_shape=jax.ShapeDtypeStruct((nctx, slots, hdim), BF16),
        in_specs=[SM] * 3 + [VM] * 8,
        out_specs=VM,
        scratch_shapes=[table[0], pltpu.VMEM((total + slots, hdim), F32)]
        + table[1:]
        + [
            table[1],
            pltpu.VMEM((hdim, total), BF16),
            pltpu.VMEM((1, total), F32),
            pltpu.VMEM((1, total), F32),
        ],
        compiler_params=params,
        name="grads",
    )(before, here_vec, head_scale, *arrays, got_rest, att, lse, delta)
    groups = [[i for i in range(nctx) if i // 2 % 2 == j] for j in range(2)]
    dsc = lax.all_to_all(
        dsc,
        "ctx",
        split_axis=0,
        concat_axis=0,
        axis_index_groups=groups,
        tiled=True,
    )
    back, dsc = lax.optimization_barrier((back, dsc))
    home = lax.all_to_all(back, "ctx", split_axis=0, concat_axis=0, tiled=True)
    dsc = lax.psum(jnp.sum(dsc, axis=0)[:, :heads], "dp")
    home, dsc = lax.optimization_barrier((home, dsc))
    outs = pl.pallas_call(
        place_kernel,
        out_shape=tuple([jax.ShapeDtypeStruct((tok, width), BF16)] * 4)
        + (jax.ShapeDtypeStruct((1, tok), F32),),
        in_specs=[SM] + [VM] * 4,
        out_specs=(VM,) * 5,
        compiler_params=params,
        name="place",
    )(here_vec, routed, router_logit, grad_out[0], home)
    block_out, d_q, d_k, d_v, d_logit = outs
    return block_out[None], d_q[None], d_k[None], d_v[None], d_logit, dsc[0]


def solution(mesh):
    in_specs = (
        P("dp", "ctx", None),
        P("dp", "ctx", None),
        P("dp", "ctx", None),
        P("dp", "ctx"),
        P(),
        P("dp", None),
        P("dp", "ctx", None),
    )
    out_specs = (
        P("dp", "ctx", None),
        P("dp", "ctx", None),
        P("dp", "ctx", None),
        P("dp", "ctx", None),
        P("dp", "ctx"),
        P(),
    )
    return jax.shard_map(body, mesh=mesh, in_specs=in_specs, out_specs=out_specs, check_vma=False)
```

```python
import functools
import math

import jax
import jax.numpy as jnp
from jax import lax
from jax.experimental import pallas as pl
from jax.experimental.pallas import tpu as pltpu
from jax.sharding import PartitionSpec as P

F32 = jnp.float32
BF16 = jnp.bfloat16
VM = pl.BlockSpec(memory_space=pltpu.VMEM)
SM = pl.BlockSpec(memory_space=pltpu.SMEM)
HB = pl.BlockSpec(memory_space=pltpu.HBM)
NT = (((1,), (1,)), ((), ()))
PARTS = 4
FAR = -3e38
BLK = 256
STRIP = 32


def eye(n):
    return lax.broadcasted_iota(jnp.int32, (n, n), 0) == lax.broadcasted_iota(jnp.int32, (n, n), 1)


def to_row(col, n):
    return jnp.sum(jnp.where(eye(n), col, 0.0), axis=0, keepdims=True)


def to_col(row, n):
    return jnp.sum(jnp.where(eye(n), row, 0.0), axis=1, keepdims=True)


def slot_column(places, first, tok):
    total = places.shape[1]
    before = jnp.sum((places < first).astype(F32), axis=1, keepdims=True)
    rank = lax.broadcasted_iota(jnp.int32, (1, total), 1).astype(F32) + 1.0 - before
    here = places - first == lax.broadcasted_iota(jnp.int32, (tok, total), 0)
    return jnp.sum(jnp.where(here, rank, 0.0), axis=1, keepdims=True)


def sigmoid(x):
    return 1.0 / (1.0 + jnp.exp(-x))


def pack_kernel(
    here_ref, places_hbm, logit_hbm, q_hbm, k_hbm, v_hbm, g_hbm, out_ref, places, logit, buf, sems
):
    tok, width = q_hbm.shape
    slots, hdim = out_ref.shape[1:]
    small = [
        pltpu.make_async_copy(src, dst, sems.at[PARTS + i])
        for i, (src, dst) in enumerate(((places_hbm, places), (logit_hbm, logit)))
    ]
    copies = [
        pltpu.make_async_copy(ref, buf.at[part], sems.at[part])
        for part, ref in enumerate((q_hbm, k_hbm, v_hbm, g_hbm))
    ]
    for copy in small + copies:
        copy.start()
    for copy in small:
        copy.wait()
    row = to_row(slot_column(places[...], here_ref[0] * tok, tok), tok)
    hit = lax.broadcasted_iota(jnp.int32, (slots, tok), 0).astype(F32) + 1.0 == row
    pick = hit.astype(BF16)
    gate = jnp.sum(jnp.where(hit, sigmoid(logit[...]), 0.0), axis=1, keepdims=True)
    for part, copy in enumerate(copies):
        copy.wait()
        for base in range(0, width, 4 * hdim):
            rows = jnp.dot(pick, buf[part, :, base : base + 4 * hdim], preferred_element_type=F32)
            if part == 3:
                rows = rows * gate
            rows = rows.astype(BF16)
            for i in range(4):
                head = base // hdim + i
                out_ref[head * PARTS + part] = rows[:, i * hdim : (i + 1) * hdim]


def compact_kernel(before_ref, in_ref, out_ref, buf):
    shards, slots, _ = in_ref.shape
    total = out_ref.shape[0]
    for c in range(shards):
        buf[pl.ds(before_ref[c], slots), :] = in_ref[c].astype(F32)
    out_ref[...] = buf[:total, :].astype(BF16)


def fold(x, op):
    return op(x.reshape(x.shape[0] // 8, 8, x.shape[1]), axis=0)


def strips(lo):
    return [slice(a, a + STRIP) for a in range(0, lo + BLK, STRIP)]


def raw_scores(k_ref, q_ref, rbuf, lo):
    n = lo + BLK
    raw = lax.dot_general(k_ref[:n, :], q_ref[lo:n, :], NT, preferred_element_type=F32)
    tri = lax.broadcasted_iota(jnp.int32, (BLK, BLK), 0) <= lax.broadcasted_iota(
        jnp.int32, (BLK, BLK), 1
    )
    if lo:
        rbuf[:lo, lo:n] = raw[:lo, :]
    rbuf[lo:n, lo:n] = jnp.where(tri, raw[lo:, :], FAR)


def products(v_ref, g_ref, gbuf, lo):
    n = lo + BLK
    gbuf[:n, lo:n] = lax.dot_general(v_ref[:n, :], g_ref[lo:n, :], NT, preferred_element_type=F32)


def forward(refs, rbuf, pbuf, gbuf, coef2, att_ref, lse_ref, delta_ref):
    q_ref, k_ref, v_ref, g_ref = refs
    blocks = range(0, q_ref.shape[0], BLK)
    for lo in blocks:
        raw_scores(k_ref, q_ref, rbuf, lo)
    vt = v_ref[...].astype(F32).T.astype(BF16)
    lses = []
    for lo in blocks:
        cols = slice(lo, lo + BLK)
        top = jnp.full((8, BLK), -jnp.inf, F32)
        for rows in strips(lo):
            top = jnp.maximum(top, fold(rbuf[rows, cols], jnp.max))
        top = jnp.max(top, axis=0, keepdims=True) * coef2
        acc = jnp.zeros((8, BLK), F32)
        for rows in strips(lo):
            acc = acc + fold(jnp.exp2(rbuf[rows, cols] * coef2 - top), jnp.sum)
        lse = top + jnp.log2(jnp.sum(acc, axis=0, keepdims=True))
        for rows in strips(lo):
            pbuf[rows, cols] = jnp.exp2(rbuf[rows, cols] * coef2 - lse).astype(BF16)
        lse_ref[:, cols] = lse
        lses.append(lse)
        products(v_ref, g_ref, gbuf, lo)
    deltas = []
    for lo in blocks:
        n = lo + BLK
        att = jnp.dot(vt[:, :n], pbuf[:n, lo:n], preferred_element_type=F32).astype(BF16)
        att_ref[:, lo:n] = att
        git = g_ref[lo:n, :].astype(F32).T
        delta = jnp.sum(git * att.astype(F32), axis=0, keepdims=True)
        delta_ref[:, lo:n] = delta
        deltas.append(delta)
    return lses, deltas


def stats_kernel(
    here_ref, scale_ref, x0, x1, x2, x3, ds_ref, att_ref, lse_ref, delta_ref, rest_ref, arr, pbuf, rbuf, gbuf
):
    total, hdim = x0.shape
    inv = 1.0 / math.sqrt(hdim)
    ds_ref[...] = jnp.zeros_like(ds_ref)

    @pl.when(lax.rem(here_ref[0], 2) == 0)
    def _():
        role = lax.rem(here_ref[0], PARTS)
        head = lax.div(here_ref[0], PARTS)
        for i, ref in enumerate((x0, x1, x2, x3)):
            arr[role ^ i] = ref[...]
        rest_ref[0] = x2[...]
        rest_ref[1] = x3[...]
        coef2 = scale_ref[head] * (inv * math.log2(math.e))
        refs = [arr.at[i] for i in range(PARTS)]
        lses, deltas = forward(refs, rbuf, pbuf, gbuf, coef2, att_ref, lse_ref, delta_ref)
        dsc = jnp.zeros((8, BLK), F32)
        for lo, lse, delta in zip(range(0, total, BLK), lses, deltas):
            cols = slice(lo, lo + BLK)
            for rows in strips(lo):
                raw = rbuf[rows, cols]
                ds = jnp.exp2(raw * coef2 - lse) * (gbuf[rows, cols] - delta)
                dsc = dsc + fold(ds * raw, jnp.sum)
        mine = lax.broadcasted_iota(jnp.int32, ds_ref.shape, 2) == head
        dsum = jnp.sum(jnp.sum(dsc, axis=0, keepdims=True), axis=1, keepdims=True) * inv
        ds_ref[...] = jnp.where(mine, dsum.reshape(1, 1, 1), 0.0)


def grads_kernel(
    before_ref, here_ref, scale_ref, x0, x1, x2, x3, got, att_ref, lse_ref, delta_ref, places_ref, logit_ref,
    out_ref, spread_ref, gate_ref, slope_ref,
    arr, res, pbuf, rbuf, gbuf, wbuf, att_own, lse_own, delta_own,
):
    shards, slots, hdim = out_ref.shape
    total = x0.shape[0]
    inv = 1.0 / math.sqrt(hdim)
    role = lax.rem(here_ref[0], PARTS)
    coef = scale_ref[lax.div(here_ref[0], PARTS)] * inv
    coef2 = coef * math.log2(math.e)
    blocks = range(0, total, BLK)
    refs = [arr.at[i] for i in range(PARTS)]
    q_ref, k_ref, v_ref, g_ref = refs
    arr[role] = x0[...]
    arr[role ^ 1] = x1[...]
    tok = spread_ref.shape[0]
    col = slot_column(places_ref[...], here_ref[0] * tok, tok)
    slot = lax.broadcasted_iota(jnp.int32, (tok, slots), 1).astype(F32) + 1.0
    spread_ref[...] = (slot == col).astype(BF16)
    row = sigmoid(logit_ref[...])
    gate_ref[...] = jnp.broadcast_to(to_col(row, tok), gate_ref.shape)
    slope_ref[...] = row * (1.0 - row)

    def fill(lse_of, delta_of):
        for lo in blocks:
            cols = slice(lo, lo + BLK)
            lse = lse_of[:, cols]
            delta = delta_of[:, cols]
            for rows in strips(lo):
                p = jnp.exp2(rbuf[rows, cols] * coef2 - lse)
                wbuf[rows, cols] = (p * (gbuf[rows, cols] - delta)).astype(BF16)

    @pl.when(role == 0)
    def _():
        res[:total, :] = att_ref[...].astype(F32).T

    @pl.when(role == 2)
    def _():
        arr[role ^ 2] = x2[...]
        arr[role ^ 3] = x3[...]
        for lo in blocks:
            raw_scores(k_ref, q_ref, rbuf, lo)
            products(v_ref, g_ref, gbuf, lo)
        fill(lse_ref, delta_ref)
        for lo in blocks:
            res[lo : lo + BLK, :] = coef * jnp.dot(
                wbuf[lo : lo + BLK, lo:], q_ref[lo:, :], preferred_element_type=F32
            )

    @pl.when(lax.rem(role, 2) == 1)
    def _():
        arr[role ^ 2] = got[1]
        arr[role ^ 3] = got[0]
        forward(refs, rbuf, pbuf, gbuf, coef2, att_own, lse_own, delta_own)

    @pl.when(role == 1)
    def _():
        fill(lse_own, delta_own)
        kt = k_ref[...].astype(F32).T.astype(BF16)
        for lo in blocks:
            n = lo + BLK
            dq = jnp.dot(kt[:, :n], wbuf[:n, lo:n], preferred_element_type=F32)
            res[lo:n, :] = (coef * dq).T

    @pl.when(role == 3)
    def _():
        for lo in blocks:
            res[lo : lo + BLK, :] = jnp.dot(
                pbuf[lo : lo + BLK, lo:], g_ref[lo:, :], preferred_element_type=F32
            )

    res[total:, :] = jnp.zeros((slots, hdim), F32)
    for c in range(shards):
        out_ref[c] = res[pl.ds(before_ref[c], slots), :].astype(BF16)


def place_kernel(
    spread_ref, gate_ref, slope_ref, g_ref, in_ref, bo_ref, dq_ref, dk_ref, dv_ref, dl_ref
):
    tok, width = g_ref.shape
    hdim = in_ref.shape[2]
    spread = spread_ref[...]
    gate = gate_ref[...]
    acc = jnp.zeros((tok, 2 * hdim), F32)
    for head in range(0, width // hdim, 2):
        cols = slice(head * hdim, (head + 2) * hdim)

        def home(part):
            pair = [in_ref[(head + i) * PARTS + part] for i in range(2)]
            return jnp.dot(spread, jnp.concatenate(pair, axis=1), preferred_element_type=F32)

        att = home(0)
        bo_ref[:, cols] = (gate * att).astype(BF16)
        acc = acc + g_ref[:, cols].astype(F32) * att
        dq_ref[:, cols] = home(1).astype(BF16)
        dk_ref[:, cols] = home(2).astype(BF16)
        dv_ref[:, cols] = home(3).astype(BF16)
    dot = to_row(jnp.sum(acc, axis=1, keepdims=True), tok)
    dl_ref[...] = slope_ref[...] * dot


def body(queries, keys, values, router_logit, head_scale, routed, grad_out):
    nctx = lax.axis_size("ctx")
    here = lax.axis_index("ctx")
    tok, width = queries.shape[1:]
    heads = head_scale.shape[0]
    hdim = width // heads
    total = routed.shape[1]
    rows = total // nctx
    slots = rows + 3 * (rows // 2)
    here_vec = here.astype(jnp.int32)[None]
    starts = jnp.arange(nctx, dtype=jnp.int32) * tok
    before = jnp.sum((routed[0][None, :] < starts[:, None]).astype(jnp.int32), axis=1)
    params = pltpu.CompilerParams(vmem_limit_bytes=24 * 1024 * 1024)

    send = pl.pallas_call(
        pack_kernel,
        out_shape=jax.ShapeDtypeStruct((nctx, slots, hdim), BF16),
        in_specs=[SM] + [HB] * 6,
        out_specs=VM,
        scratch_shapes=[
            pltpu.VMEM((1, total), jnp.int32),
            pltpu.VMEM((1, tok), F32),
            pltpu.VMEM((PARTS, tok, width), BF16),
            pltpu.SemaphoreType.DMA((PARTS + 2,)),
        ],
        compiler_params=pltpu.CompilerParams(vmem_limit_bytes=60 * 1024 * 1024),
        name="pack",
    )(here_vec, routed, router_logit, queries[0], keys[0], values[0], grad_out[0])
    got = lax.all_to_all(send, "ctx", split_axis=0, concat_axis=0, tiled=True)
    own = pl.pallas_call(
        compact_kernel,
        out_shape=jax.ShapeDtypeStruct((total, hdim), BF16),
        in_specs=[SM, VM],
        out_specs=VM,
        scratch_shapes=[pltpu.VMEM((total + slots, hdim), F32)],
        compiler_params=params,
        name="compact",
    )(before, got)
    odd = list(range(1, nctx, 2))
    even = list(range(0, nctx, 2))
    side = lax.ppermute(own, "ctx", [(i, i ^ 2) for i in even])
    cross = lax.ppermute(own, "ctx", [(i, i ^ 3) for i in odd])
    near = lax.ppermute(own, "ctx", [(i, i ^ 1) for i in range(nctx)])
    arrays = (own, near, side, cross)
    table = [
        pltpu.VMEM((PARTS, total, hdim), BF16),
        pltpu.VMEM((total, total), BF16),
        pltpu.VMEM((total, total), F32),
        pltpu.VMEM((total, total), F32),
    ]
    dsc, att, lse, delta, rest = pl.pallas_call(
        stats_kernel,
        out_shape=(
            jax.ShapeDtypeStruct((nctx // 2, 1, 128), F32),
            jax.ShapeDtypeStruct((hdim, total), BF16),
            jax.ShapeDtypeStruct((1, total), F32),
            jax.ShapeDtypeStruct((1, total), F32),
            jax.ShapeDtypeStruct((2, total, hdim), BF16),
        ),
        in_specs=[SM] * 2 + [VM] * 4,
        out_specs=(VM,) * 5,
        scratch_shapes=table,
        compiler_params=params,
        name="stats",
    )(here_vec, head_scale, *arrays)
    got_rest = lax.ppermute(rest, "ctx", [(i, i ^ 1) for i in even])
    back, spread, gates, slope = pl.pallas_call(
        grads_kernel,
        out_shape=(
            jax.ShapeDtypeStruct((nctx, slots, hdim), BF16),
            jax.ShapeDtypeStruct((tok, slots), BF16),
            jax.ShapeDtypeStruct((tok, 2 * hdim), F32),
            jax.ShapeDtypeStruct((1, tok), F32),
        ),
        in_specs=[SM] * 3 + [VM] * 10,
        out_specs=(VM,) * 4,
        scratch_shapes=[table[0], pltpu.VMEM((total + slots, hdim), F32)]
        + table[1:]
        + [
            table[1],
            pltpu.VMEM((hdim, total), BF16),
            pltpu.VMEM((1, total), F32),
            pltpu.VMEM((1, total), F32),
        ],
        compiler_params=params,
        name="grads",
    )(before, here_vec, head_scale, *arrays, got_rest, att, lse, delta, routed, router_logit)
    groups = [[i for i in range(nctx) if i // 2 % 2 == j] for j in range(2)]
    dsc = lax.all_to_all(
        dsc,
        "ctx",
        split_axis=0,
        concat_axis=0,
        axis_index_groups=groups,
        tiled=True,
    )
    back, dsc = lax.optimization_barrier((back, dsc))
    home = lax.all_to_all(back, "ctx", split_axis=0, concat_axis=0, tiled=True)
    dsc = lax.psum(jnp.sum(dsc, axis=0)[:, :heads], "dp")
    home, dsc = lax.optimization_barrier((home, dsc))
    outs = pl.pallas_call(
        place_kernel,
        out_shape=tuple([jax.ShapeDtypeStruct((tok, width), BF16)] * 4)
        + (jax.ShapeDtypeStruct((1, tok), F32),),
        in_specs=[VM] * 5,
        out_specs=(VM,) * 5,
        compiler_params=params,
        name="place",
    )(spread, gates, slope, grad_out[0], home)
    block_out, d_q, d_k, d_v, d_logit = outs
    return block_out[None], d_q[None], d_k[None], d_v[None], d_logit, dsc[0]


def solution(mesh):
    in_specs = (
        P("dp", "ctx", None),
        P("dp", "ctx", None),
        P("dp", "ctx", None),
        P("dp", "ctx"),
        P(),
        P("dp", None),
        P("dp", "ctx", None),
    )
    out_specs = (
        P("dp", "ctx", None),
        P("dp", "ctx", None),
        P("dp", "ctx", None),
        P("dp", "ctx", None),
        P("dp", "ctx"),
        P(),
    )
    return jax.shard_map(body, mesh=mesh, in_specs=in_specs, out_specs=out_specs, check_vma=False)
```
